256 devices in a mesh: dp: 4 (over y), ctx: 64 (over x, z, core).
Axes of the slice: x: 4, y: 4, z: 8, core: 2. Of those that a mesh axis runs over, the one named last changes fastest.
Arguments:
- queries: bfloat16 [2, 16384, 1024], P(None, ('dp', 'ctx')), parts along dimension 1, may hold values from -6 to 6
- keys: bfloat16 [1, 16384, 1024], P(None, ('dp', 'ctx')), parts along dimension 1, may hold values from -48 to 48
- values: bfloat16 [1, 16384, 1024], P(None, ('dp', 'ctx')), parts along dimension 1, may hold values from -48 to 48
- rates: float32 [1, 2, 16384], P(None, None, ('dp', 'ctx')), parts along dimension 2, may hold values from 0.05 to 1
- fast_weights: bfloat16 [3, 2, 512, 1024], replicated, may hold values from -0.25 to 0.25
Outputs:
- outputs: bfloat16 [2, 16384, 1024], P(None, ('dp', 'ctx')), parts along dimension 1
The draws below stay inside these ranges and needn't reach their ends.
There are 4 independent parts, one for each index of `dp`. The reference program is written for one: setup_inputs(seed, part) draws one part's arguments, and reference() takes and returns one part's arrays. A program takes and returns all parts, laid end to end along the dimension named above; an argument that names none is the same for every part. Nothing has to cross between parts.
All inputs are finite; a program needn't handle non-finite values.
Results may differ from the reference program's by a relative error of at most 0.007.
The reference program's roundings to bfloat16 on the way count: a program that leaves them out, or rounds other values in their place, can miss the bound.
Values may be sent and summed in bfloat16 or wider, within the bound.
No kernel may reach another device: no remote copies, remote signals or barrier semaphores. Data moves between devices by JAX's collectives and lax.ppermute only.
A program may use at most 128 MiB of HBM per device.

```python
import math
import jax
import jax.numpy as jnp
from jax import lax

HEADS = 2
HEAD_DIM = 512
FF = 1024
BLOCKS = 2
BLOCK = 4096
WIDTH = 1024


def feature_scales(key, rise):
    position = (jnp.arange(WIDTH) % HEAD_DIM).astype(jnp.float32) / HEAD_DIM
    jitter = jax.random.uniform(key, (WIDTH,), jnp.float32)
    return jnp.exp(math.log(rise) * (position + jitter))


def draw_keys(key, part):
    key = jax.random.fold_in(key, 17)
    col_key, tok_key, base_key = jax.random.split(key, 3)
    columns = feature_scales(col_key, 3.0)
    shape = (BLOCKS - 1, BLOCK, WIDTH)
    token_scale = jnp.exp(math.log(2.0) * jax.random.uniform(tok_key, (BLOCKS - 1, BLOCK, 1), jnp.float32))
    base = jnp.clip(jax.random.normal(base_key, shape, jnp.float32), -4.0, 4.0)
    return (base * columns * token_scale / 3.0).astype(jnp.bfloat16)


def draw_values(key, part):
    key = jax.random.fold_in(key, 29)
    col_key, tok_key, base_key = jax.random.split(key, 3)
    columns = feature_scales(col_key, 3.0)
    shape = (BLOCKS - 1, BLOCK, WIDTH)
    token_scale = jnp.exp(math.log(2.0) * jax.random.uniform(tok_key, (BLOCKS - 1, BLOCK, 1), jnp.float32))
    base = jnp.clip(jax.random.normal(base_key, shape, jnp.float32), -4.0, 4.0)
    return (base * columns * token_scale / 3.0).astype(jnp.bfloat16)


def block_scale(rng, extent, pieces, smallest, top_value):
    gain, own = 1.0, jax.random.fold_in(rng, 6)
    for dim, shards_of in pieces:
        draws = jnp.exp(jax.random.uniform(jax.random.fold_in(own, dim), (shards_of,), jnp.float32, smallest / len(pieces), top_value / len(pieces)))
        gain = gain * jnp.repeat(draws, extent[dim] // shards_of).reshape([-1 if axis == dim else 1 for axis in range(len(extent))])
    return gain


def noise(own_key, extent, spread, most, shards=(), kind=jnp.bfloat16):
    values = jax.random.normal(own_key, extent, jnp.float32) * spread
    if len(shards) > 0:
        values = block_scale(own_key, extent, shards, -0.22, 0.18) * values
    return jnp.clip(values, min=-most, max=most).astype(kind)


def setup_inputs(seed: int = 0, part: int = 0) -> dict:
    seeds = jax.random.split(jax.random.key(seed), 6)
    part_keys = jax.random.split(jax.random.fold_in(seeds[5], part), 6)
    queries = noise(part_keys[0], (BLOCKS, BLOCK, WIDTH), 1.0, 6.0, ((1, 64),))
    keys = draw_keys(jax.random.fold_in(jax.random.fold_in(seeds[5], part), 71), part)
    values = draw_values(jax.random.fold_in(jax.random.fold_in(seeds[5], part), 71), part)
    rates = jnp.clip(jnp.exp(math.log(1.0) - 2.9957323 * jax.random.uniform(part_keys[3], (BLOCKS - 1, HEADS, BLOCK), jnp.float32) ** block_scale(part_keys[3], (BLOCKS - 1, HEADS, BLOCK), ((2, 64),), -0.2, 0.2)), 0.05, 1.0)
    fast_weights = noise(seeds[4], (3, HEADS, HEAD_DIM, FF), HEAD_DIM ** -0.5, 0.25)
    return dict(queries=queries, keys=keys, values=values, rates=rates, fast_weights=fast_weights)


upd_scale = 2.0
norm_eps = 1e-07

def product(form, left, right):
    return jnp.einsum(form, left.astype(jnp.float32), right.astype(jnp.float32))

def apply_block(weights, query_block):
    row_count = query_block.shape[0]
    split_q = query_block.reshape(row_count, HEADS, HEAD_DIM)
    first_proj = product('thd,hdf->thf', split_q, weights[0])
    third_proj = product('thd,hdf->thf', split_q, weights[1])
    gated_hidden = (jax.nn.silu(first_proj) * third_proj).astype(jnp.bfloat16)
    result = product('thf,hdf->thd', gated_hidden, weights[2])
    return result.reshape(row_count, WIDTH).astype(jnp.bfloat16)

def block_gradient(weights, key_block, value_block, rate_block):
    row_count = key_block.shape[0]
    split_k = key_block.reshape(row_count, HEADS, HEAD_DIM)
    split_v = value_block.reshape(row_count, HEADS, HEAD_DIM)
    scaled_values = (split_v.astype(jnp.float32) * jnp.transpose(rate_block)[:, :, None]).astype(jnp.bfloat16)
    key_first = product('thd,hdf->thf', split_k, weights[0])
    key_third = product('thd,hdf->thf', split_k, weights[1])
    sigmoid_first = jax.nn.sigmoid(key_first)
    key_act = key_first * sigmoid_first
    key_gated = (key_act * key_third).astype(jnp.bfloat16)
    back_grad = -product('thd,hdf->thf', scaled_values, weights[2])
    d_first = (back_grad * key_third * sigmoid_first * (1.0 + key_first * (1.0 - sigmoid_first))).astype(jnp.bfloat16)
    d_third = (back_grad * key_act).astype(jnp.bfloat16)
    grad_first = product('thd,thf->hdf', split_k, d_first)
    grad_third = product('thd,thf->hdf', split_k, d_third)
    grad_down = -product('thd,thf->hdf', scaled_values, key_gated)
    return jnp.stack([grad_first, grad_third, grad_down])

def finish_full(scaled, weights):
    identity = jnp.eye(HEAD_DIM, dtype=jnp.float32)
    gram_full = product('mhdf,mhef->mhde', scaled, scaled).astype(jnp.bfloat16)
    gram_float = gram_full.astype(jnp.float32)
    gram_level = jnp.sqrt(lax.optimization_barrier(jnp.sum(gram_float * gram_float, axis=(2, 3), keepdims=True))) + norm_eps
    first_poly = (1.5 * identity - 0.5 * gram_float / gram_level).astype(jnp.bfloat16)
    squared = product('mhde,mhek->mhdk', first_poly, first_poly).astype(jnp.bfloat16)
    moved_gram = product('mhde,mhek->mhdk', squared, gram_full)
    second_poly = (1.5 * identity - 0.5 * moved_gram / gram_level).astype(jnp.bfloat16)
    combined = product('mhde,mhek->mhdk', second_poly, first_poly).astype(jnp.bfloat16)
    update = product('mhde,mhef->mhdf', combined, scaled) / jnp.sqrt(gram_level)
    return (weights.astype(jnp.float32) - upd_scale * update).astype(jnp.bfloat16)

def reference(queries, keys, values, rates, fast_weights):
    weights = fast_weights
    results = []
    for block_index in range(BLOCKS):
        results.append(apply_block(weights, queries[block_index]))
        if block_index + 1 < BLOCKS:
            grads = block_gradient(weights, keys[block_index], values[block_index], rates[block_index])
            scaled = grads.astype(jnp.bfloat16)
            weights = finish_full(scaled, weights)
    return jnp.stack(results)
```

```python
import functools

import jax
import jax.numpy as jnp
from jax import lax
from jax.experimental import pallas as pl
from jax.experimental.pallas import tpu as pltpu
from jax.sharding import PartitionSpec as P

X, Z, C = 4, 8, 2
DIM, FF, COLS = 512, 1024, 256
ROWS = DIM // Z
BF, F32 = jnp.bfloat16, jnp.float32
VMEM_LIMIT = 48 * 1024 * 1024
upd_scale = 2.0
norm_eps = 1e-07
VMEM = pl.BlockSpec(memory_space=pltpu.VMEM)
ANY = pl.BlockSpec(memory_space=pl.ANY)


def place():
    index = lax.axis_index("ctx")
    return index // (Z * C), (index // C) % Z, index % C


def move(array, to):
    perm = []
    for x in range(X):
        for z in range(Z):
            for c in range(C):
                tx, tz, tc = to(x, z, c)
                perm.append(((x * Z + z) * C + c, (tx % X * Z + tz % Z) * C + tc % C))
    return lax.ppermute(array, "ctx", perm)


def dot(left, right, dims):
    return lax.dot_general(left, right, (dims, ((), ())), preferred_element_type=F32)


def prepare_kernel(keys, values, rates, query, own, far1, far2, far3, query_own, query_far):
    x, _, _ = place()
    tokens = keys.shape[0]
    diagonal = lax.broadcasted_iota(jnp.int32, (tokens, tokens), 0) == lax.broadcasted_iota(
        jnp.int32, (tokens, tokens), 1
    )

    def fill(head):
        row = rates[head : head + 1, :]
        rate = jnp.sum(jnp.where(diagonal, row, 0.0), axis=1, keepdims=True)
        cols = slice(head * DIM, (head + 1) * DIM)
        scaled = (values[:, cols].astype(F32) * rate).astype(BF)
        for distance, ref in enumerate((own, far1, far2, far3)):

            @pl.when(lax.rem(x + distance, X) // 2 == head)
            def _():
                ref[:tokens, :] = keys[:, cols]
                ref[tokens:, :] = scaled

        @pl.when(x // 2 == head)
        def _():
            query_own[...] = query[:, cols]

        @pl.when(x // 2 != head)
        def _():
            query_far[...] = query[:, cols]

    fill(0)
    fill(1)


def prepare(keys, values, rates, query):
    tokens = keys.shape[0]
    pair = jax.ShapeDtypeStruct((2 * tokens, DIM), BF)
    half = jax.ShapeDtypeStruct((tokens, DIM), BF)
    return pl.pallas_call(
        prepare_kernel,
        out_shape=(pair, pair, pair, pair, half, half),
        in_specs=[VMEM] * 4,
        out_specs=(VMEM,) * 6,
        name="prepare",
    )(keys, values, rates, query)


def gradient_kernel(*refs):
    pieces, weights = refs[:8], refs[8]
    outs = refs[9:17]
    w, k, v, total, sem = refs[17:]
    x, z, c = place()
    column = pl.multiple_of((lax.rem(x, 2) * 2 + c) * COLS, COLS)
    copies = []
    for m in range(3):
        copy = pltpu.make_async_copy(
            weights.at[m, x // 2, :, pl.ds(column, COLS)], w.at[m], sem.at[m]
        )
        copy.start()
        copies.append(copy)
    tokens = pieces[0].shape[0] // 2
    for i, piece in enumerate(pieces):
        k[i * tokens : (i + 1) * tokens, :] = piece[:tokens, :]
        v[i * tokens : (i + 1) * tokens, :] = piece[tokens:, :]
    for copy in copies:
        copy.wait()
    key_first = dot(k[...], w[0], ((1,), (0,)))
    key_third = dot(k[...], w[1], ((1,), (0,)))
    back_grad = -dot(v[...], w[2], ((1,), (0,)))
    sig = jax.nn.sigmoid(key_first)
    key_act = key_first * sig
    key_gated = (key_act * key_third).astype(BF)
    d_first = (back_grad * key_third * sig * (1.0 + key_first * (1.0 - sig))).astype(BF)
    d_third = (back_grad * key_act).astype(BF)
    total[0] = dot(k[...], d_first, ((0,), (0,)))
    total[1] = dot(k[...], d_third, ((0,), (0,)))
    total[2] = -dot(v[...], key_gated, ((0,), (0,)))
    for distance in range(Z):
        row = pl.multiple_of(lax.rem(z + distance, Z) * ROWS, ROWS)
        for m in range(3):
            outs[distance][m] = total[m, pl.ds(row, ROWS), :].astype(outs[distance].dtype)


def gradient(pieces, weights):
    tokens = 8 * pieces[0].shape[0] // 2
    out_shape = [jax.ShapeDtypeStruct((3, ROWS, COLS), F32 if d == 0 else BF) for d in range(Z)]
    return pl.pallas_call(
        gradient_kernel,
        out_shape=out_shape,
        in_specs=[VMEM] * 8 + [ANY],
        out_specs=[VMEM] * Z,
        scratch_shapes=[
            pltpu.VMEM((3, DIM, COLS), BF),
            pltpu.VMEM((tokens, DIM), BF),
            pltpu.VMEM((tokens, DIM), BF),
            pltpu.VMEM((3, DIM, COLS), F32),
            pltpu.SemaphoreType.DMA((3,)),
        ],
        compiler_params=pltpu.CompilerParams(vmem_limit_bytes=VMEM_LIMIT),
        cost_estimate=pl.CostEstimate(
            flops=12 * tokens * DIM * COLS, bytes_accessed=4 << 20, transcendentals=tokens * COLS
        ),
        name="gradient",
    )(*pieces, weights)


def renew_kernel(*refs):
    pieces, weights, query_own, query_far = refs[:32], refs[32], refs[33], refs[34]
    out_own, out_far = refs[35], refs[36]
    scaled, w, sem, wsem = refs[37:]
    x, z, c = place()
    copies = []
    for i in range(4):
        part = lax.rem(x + i // 2, 2) * 2 + lax.rem(c + i % 2, 2)
        for distance in range(Z):
            row = pl.multiple_of(lax.rem(z - distance + Z, Z) * ROWS, ROWS)
            copy = pltpu.make_async_copy(
                pieces[i * Z + distance],
                scaled.at[part, :, pl.ds(row, ROWS), :],
                sem.at[i * Z + distance],
            )
            copy.start()
            copies.append(copy)
    load = pltpu.make_async_copy(weights.at[:, x // 2], w, wsem)
    load.start()
    for copy in copies:
        copy.wait()
    load.wait()
    identity = (
        lax.broadcasted_iota(jnp.int32, (DIM, DIM), 0)
        == lax.broadcasted_iota(jnp.int32, (DIM, DIM), 1)
    ).astype(F32)

    @pl.loop(0, 3)
    def _(m):
        gram = dot(scaled[0, m], scaled[0, m], ((1,), (1,)))
        for part in range(1, 4):
            gram += dot(scaled[part, m], scaled[part, m], ((1,), (1,)))
        gram = gram.astype(BF)
        gram_float = gram.astype(F32)
        level = jnp.sqrt(jnp.sum(gram_float * gram_float, keepdims=True)) + norm_eps
        half = 0.5 / level
        first_poly = (1.5 * identity - gram_float * half).astype(BF)
        squared = dot(first_poly, first_poly, ((1,), (0,))).astype(BF)
        moved = dot(squared, gram, ((1,), (0,)))
        second_poly = (1.5 * identity - moved * half).astype(BF)
        combined = dot(second_poly, first_poly, ((1,), (0,))).astype(BF)
        factor = upd_scale / jnp.sqrt(level)
        for part in range(4):
            cols = slice(part * COLS, (part + 1) * COLS)
            update = dot(combined, scaled[part, m], ((1,), (0,))) * factor
            w[m, :, cols] = (w[m, :, cols].astype(F32) - update).astype(BF)

    query = jnp.concatenate([query_own[...], query_far[...]], axis=0)
    first_proj = dot(query, w[0], ((1,), (0,)))
    third_proj = dot(query, w[1], ((1,), (0,)))
    gated = (first_proj * jax.nn.sigmoid(first_proj) * third_proj).astype(BF)
    result = dot(gated, w[2], ((1,), (1,))).astype(BF)
    tokens = query_own.shape[0]
    out_own[...] = result[:tokens]
    out_far[...] = result[tokens:]


def renew_apply(pieces, weights, query_own, query_far):
    half = jax.ShapeDtypeStruct(query_own.shape, BF)
    return pl.pallas_call(
        renew_kernel,
        out_shape=(half, half),
        in_specs=[ANY] * 33 + [VMEM] * 2,
        out_specs=(VMEM, VMEM),
        scratch_shapes=[
            pltpu.VMEM((4, 3, DIM, COLS), BF),
            pltpu.VMEM((3, DIM, FF), BF),
            pltpu.SemaphoreType.DMA((32,)),
            pltpu.SemaphoreType.DMA,
        ],
        compiler_params=pltpu.CompilerParams(vmem_limit_bytes=VMEM_LIMIT),
        cost_estimate=pl.CostEstimate(
            flops=6 * 10**9, bytes_accessed=7 << 20, transcendentals=1 << 17
        ),
        name="renew_apply",
    )(*pieces, weights, query_own, query_far)


def apply_block(weights, query):
    tokens = query.shape[0]
    split_q = query.reshape(tokens, 2, DIM)
    first_proj = jnp.einsum("thd,hdf->thf", split_q, weights[0], preferred_element_type=F32)
    third_proj = jnp.einsum("thd,hdf->thf", split_q, weights[1], preferred_element_type=F32)
    gated_hidden = (jax.nn.silu(first_proj) * third_proj).astype(BF)
    result = jnp.einsum("thf,hdf->thd", gated_hidden, weights[2], preferred_element_type=F32)
    return result.reshape(tokens, 2 * DIM).astype(BF)


def body(queries, keys, values, rates, weights):
    own, far1, far2, far3, query_own, query_far = prepare(keys[0], values[0], rates[0], queries[1])
    got = [own]
    for distance, payload in ((1, far1), (2, far2), (3, far3)):
        got.append(move(payload, lambda x, z, c: (x + distance, z, c)))
    got += [move(piece, lambda x, z, c: (x, z, c + 1)) for piece in got]
    query_got = move(query_far, lambda x, z, c: (X - 1 - x, z, c))
    chunks = gradient(got, weights)
    query_zero, chunks = lax.optimization_barrier((queries[0], chunks))
    total = chunks[0]
    for distance in (4, 3, 5, 2, 6, 1, 7):
        total = total + move(chunks[distance], lambda x, z, c: (x, z + distance, c)).astype(F32)
    scaled = total.astype(BF)
    first_out = apply_block(weights, query_zero)
    mine = [scaled] + [move(scaled, lambda x, z, c: (x, z + d, c)) for d in range(1, Z)]
    near = [move(piece, lambda x, z, c: (x, z, c + 1)) for piece in mine]
    across = [move(piece, lambda x, z, c: (x ^ 1, z, c)) for piece in mine]
    last = [move(piece, lambda x, z, c: (x, z, c + 1)) for piece in across]
    out_own, out_far = renew_apply(mine + near + across + last, weights, query_own, query_got)
    out_got = move(out_far, lambda x, z, c: (X - 1 - x, z, c))
    x, _, _ = place()
    second_out = jnp.where(
        x // 2 == 0,
        jnp.concatenate([out_own, out_got], axis=1),
        jnp.concatenate([out_got, out_own], axis=1),
    )
    return jnp.stack([first_out, second_out])


def solution(mesh):
    in_specs = (
        P(None, ("dp", "ctx"), None),
        P(None, ("dp", "ctx"), None),
        P(None, ("dp", "ctx"), None),
        P(None, None, ("dp", "ctx")),
        P(),
    )
    out_specs = P(None, ("dp", "ctx"), None)
    return jax.shard_map(body, mesh=mesh, in_specs=in_specs, out_specs=out_specs, check_vma=False)
```

```python
import jax
import jax.numpy as jnp
from jax import lax
from jax.experimental import pallas as pl
from jax.experimental.pallas import tpu as pltpu
from jax.sharding import PartitionSpec as P

X, Z, C = 4, 8, 2
DIM, FF = 512, 1024
HALF, QUARTER = FF // 2, FF // 4
WIDE = HALF + QUARTER
ROWS = DIM // Z
BF, F32 = jnp.bfloat16, jnp.float32
VMEM_LIMIT = 48 * 1024 * 1024
upd_scale = 2.0
norm_eps = 1e-07
VMEM = pl.BlockSpec(memory_space=pltpu.VMEM)
ANY = pl.BlockSpec(memory_space=pl.ANY)


def place():
    index = lax.axis_index("ctx")
    return index // (Z * C), (index // C) % Z, index % C


def move(array, to):
    perm = []
    for x in range(X):
        for z in range(Z):
            for c in range(C):
                tx, tz, tc = to(x, z, c)
                perm.append(((x * Z + z) * C + c, (tx % X * Z + tz % Z) * C + tc % C))
    return lax.ppermute(array, "ctx", perm)


def along_x(array, distance):
    return move(array, lambda x, z, c: (x + distance, z, c))


def along_z(array, distance):
    return move(array, lambda x, z, c: (x, z + distance, c))


def pair_x(array):
    return move(array, lambda x, z, c: (x ^ 1, z, c))


def mirror_x(array):
    return move(array, lambda x, z, c: (X - 1 - x, z, c))


def mirror_x_core(array):
    return move(array, lambda x, z, c: (X - 1 - x, z, c + 1))


def other_core(array):
    return move(array, lambda x, z, c: (x, z, c + 1))


def dot(left, right, dims):
    return lax.dot_general(left, right, (dims, ((), ())), preferred_element_type=F32)


def shape(*dims, dtype=BF):
    return jax.ShapeDtypeStruct(dims, dtype)


def params():
    return pltpu.CompilerParams(vmem_limit_bytes=VMEM_LIMIT)


def cost(flops, size):
    return pl.CostEstimate(flops=flops, bytes_accessed=size, transcendentals=0)


def at_place(start, size):
    return pl.ds(pl.multiple_of(start, size), size)


def prepare_kernel(queries, keys, values, rates, own, far1, far2, far3, query_own, query_far):
    x, _, _ = place()
    tokens = keys.shape[1]
    diagonal = lax.broadcasted_iota(jnp.int32, (tokens, tokens), 0) == lax.broadcasted_iota(
        jnp.int32, (tokens, tokens), 1
    )
    for head in range(2):
        row = rates[0, head : head + 1, :]
        rate = jnp.sum(jnp.where(diagonal, row, 0.0), axis=1, keepdims=True)
        cols = slice(head * DIM, (head + 1) * DIM)
        scaled = (values[0, :, cols].astype(F32) * rate).astype(BF)
        for distance, ref in enumerate((own, far1, far2, far3)):

            @pl.when(lax.rem(x + distance, X) // 2 == head)
            def _():
                ref[:tokens, :] = keys[0, :, cols]
                ref[tokens:, :] = scaled

        @pl.when(x // 2 == head)
        def _():
            query_own[...] = queries[1, :, cols]

        @pl.when(x // 2 != head)
        def _():
            query_far[...] = queries[1, :, cols]


def prepare(queries, keys, values, rates):
    tokens = keys.shape[1]
    pair, half = shape(2 * tokens, DIM), shape(tokens, DIM)
    return pl.pallas_call(
        prepare_kernel,
        out_shape=(pair, pair, pair, pair, half, half),
        in_specs=[VMEM] * 4,
        out_specs=(VMEM,) * 6,
        name="prepare",
    )(queries, keys, values, rates)


def first_kernel(queries, weights, out, w, sem):
    copies = []
    for head in range(2):
        for m in range(3):
            copy = pltpu.make_async_copy(weights.at[m, head], w.at[head, m], sem.at[head, m])
            copy.start()
            copies.append(copy)
    for head in range(2):
        cols = slice(head * DIM, (head + 1) * DIM)
        query = queries[0, :, cols]
        copies[3 * head].wait()
        first_proj = dot(query, w[head, 0], ((1,), (0,)))
        copies[3 * head + 1].wait()
        third_proj = dot(query, w[head, 1], ((1,), (0,)))
        gated = (first_proj * jax.nn.sigmoid(first_proj) * third_proj).astype(BF)
        copies[3 * head + 2].wait()
        out[:, cols] = dot(gated, w[head, 2], ((1,), (1,))).astype(BF)


def first_block(queries, weights):
    tokens = queries.shape[1]
    return pl.pallas_call(
        first_kernel,
        out_shape=shape(tokens, 2 * DIM),
        in_specs=[VMEM, ANY],
        out_specs=VMEM,
        scratch_shapes=[pltpu.VMEM((2, 3, DIM, FF), BF), pltpu.SemaphoreType.DMA((2, 3))],
        compiler_params=params(),
        cost_estimate=cost(12 * tokens * DIM * FF, 7 << 20),
        name="first_block",
    )(queries, weights)


def gradient_kernel(*refs):
    pieces, weights = refs[:8], refs[8]
    own, near_up, near_down, keep_up, keep_down, send_up, send_down, far_up, far_down = refs[9:18]
    w, k, v, d, gated, total, sem = refs[18:]
    x, z, c = place()
    copies = []
    for m in range(3):
        copy = pltpu.make_async_copy(
            weights.at[m, x // 2, :, at_place(lax.rem(x, 2) * HALF, HALF)], w.at[m], sem.at[m]
        )
        copy.start()
        copies.append(copy)
    tokens = pieces[0].shape[0] // 2
    for i, piece in enumerate(pieces):
        k[i * tokens : (i + 1) * tokens, :] = piece[:tokens, :]
        v[i * tokens : (i + 1) * tokens, :] = piece[tokens:, :]
    for copy in copies:
        copy.wait()
    key_first = dot(k[...], w[0], ((1,), (0,)))
    key_third = dot(k[...], w[1], ((1,), (0,)))
    back_grad = -dot(v[...], w[2], ((1,), (0,)))
    sig = jax.nn.sigmoid(key_first)
    key_act = key_first * sig

    @pl.when(c == 0)
    def _():
        d[...] = (back_grad * key_third * sig * (1.0 + key_first * (1.0 - sig))).astype(BF)
        gated[...] = (key_act[:, :QUARTER] * key_third[:, :QUARTER]).astype(BF)

    @pl.when(c == 1)
    def _():
        d[...] = (back_grad * key_act).astype(BF)
        gated[...] = (key_act[:, QUARTER:] * key_third[:, QUARTER:]).astype(BF)

    total[:, :HALF] = dot(k[...], d[...], ((0,), (0,)))
    total[:, HALF:] = -dot(v[...], gated[...], ((0,), (0,)))

    def rows(distance):
        return total[at_place(lax.rem(z + distance + Z, Z) * ROWS, ROWS), :]

    own[...] = rows(0)
    near_up[...] = rows(1).astype(BF)
    near_down[...] = rows(-1).astype(BF)
    keep_up[...] = rows(2)
    keep_down[...] = rows(-2)
    send_up[...] = rows(3).astype(BF)
    send_down[...] = rows(-3).astype(BF)
    far = rows(4).astype(BF)
    far_up[...] = far[: ROWS // 2]
    far_down[...] = far[ROWS // 2 :]


def gradient(pieces, weights):
    tokens = 8 * pieces[0].shape[0] // 2
    kept, sent, half = shape(ROWS, WIDE, dtype=F32), shape(ROWS, WIDE), shape(ROWS // 2, WIDE)
    return pl.pallas_call(
        gradient_kernel,
        out_shape=(kept, sent, sent, kept, kept, sent, sent, half, half),
        in_specs=[VMEM] * 8 + [ANY],
        out_specs=(VMEM,) * 9,
        scratch_shapes=[
            pltpu.VMEM((3, DIM, HALF), BF),
            pltpu.VMEM((tokens, DIM), BF),
            pltpu.VMEM((tokens, DIM), BF),
            pltpu.VMEM((tokens, HALF), BF),
            pltpu.VMEM((tokens, QUARTER), BF),
            pltpu.VMEM((DIM, WIDE), F32),
            pltpu.SemaphoreType.DMA((3,)),
        ],
        compiler_params=params(),
        cost_estimate=cost(10 * tokens * DIM * HALF, 6 << 20),
        name="gradient",
    )(*pieces, weights)


def middle_kernel(keep_up, keep_down, got_up, got_down, far_up, far_down, up, down):
    half = ROWS // 2
    total = keep_up[...] + got_up[...].astype(F32)
    up[:half, :] = (total[:half] + far_up[...].astype(F32)).astype(BF)
    up[half:, :] = total[half:].astype(BF)
    total = keep_down[...] + got_down[...].astype(F32)
    down[:half, :] = total[:half].astype(BF)
    down[half:, :] = (total[half:] + far_down[...].astype(F32)).astype(BF)


def middle(*args):
    return pl.pallas_call(
        middle_kernel,
        out_shape=(shape(ROWS, WIDE), shape(ROWS, WIDE)),
        in_specs=[VMEM] * 6,
        out_specs=(VMEM, VMEM),
        name="middle",
    )(*args)


def total_kernel(own, a, b, c, d, out):
    total = own[...] + a[...].astype(F32) + b[...].astype(F32) + c[...].astype(F32)
    out[...] = (total + d[...].astype(F32)).astype(BF)


def add_up(*args):
    return pl.pallas_call(
        total_kernel,
        out_shape=shape(ROWS, WIDE),
        in_specs=[VMEM] * 5,
        out_specs=VMEM,
        name="add_up",
    )(*args)


def reduce_rows(parts):
    own, near_up, near_down, keep_up, keep_down, send_up, send_down, far_up, far_down = parts
    far_up, far_down = along_z(far_up, 2), along_z(far_down, -2)
    got_up, got_down = along_z(send_up, 1), along_z(send_down, -1)
    near_up, near_down = along_z(near_up, 1), along_z(near_down, -1)
    up, down = middle(keep_up, keep_down, got_up, got_down, far_up, far_down)
    up, down = along_z(up, 2), along_z(down, -2)
    return add_up(own, near_up, near_down, up, down)


ORIGINS = ((0, 0, ROWS), (-1, 0, ROWS), (1, 0, ROWS), (-2, 0, ROWS), (2, 0, ROWS)) + (
    (-3, 0, ROWS),
    (3, 0, ROWS),
    (-4, 0, ROWS // 2),
    (4, ROWS // 2, ROWS // 2),
)


def gather_rows(own):
    up1, down1 = along_z(own, 1), along_z(own, -1)
    up2, down2 = along_z(own, 2), along_z(own, -2)
    up3, down3 = along_z(up2, 1), along_z(down2, -1)
    up4, down4 = along_z(up2[: ROWS // 2], 2), along_z(down2[ROWS // 2 :], -2)
    pieces = [own, up1, down1, up2, down2, up3, down3, up4, down4]
    return pieces + [pair_x(piece) for piece in pieces]


def pack_kernel(*refs):
    pieces = refs[:18]
    matrix, shared, sem = refs[18:]
    x, z, _ = place()
    copies = []
    for i, piece in enumerate(pieces):
        side = lax.rem(x + i // 9, 2)
        step, first, count = ORIGINS[i % 9]
        start = lax.rem(z + step + Z, Z) * ROWS + first
        rows = at_place(start, count)
        for j, (target, size, offset) in enumerate(((matrix, HALF, 0), (shared, QUARTER, HALF))):
            copy = pltpu.make_async_copy(
                piece.at[:, pl.ds(offset, size)],
                target.at[rows, at_place(side * size, size)],
                sem.at[i, j],
            )
            copy.start()
            copies.append(copy)
    for copy in copies:
        copy.wait()


def pack(pieces):
    return pl.pallas_call(
        pack_kernel,
        out_shape=(shape(DIM, FF), shape(DIM, HALF)),
        in_specs=[ANY] * 18,
        out_specs=(VMEM, VMEM),
        scratch_shapes=[pltpu.SemaphoreType.DMA((18, 2))],
        compiler_params=params(),
        cost_estimate=cost(0, 3 << 20),
        name="pack",
    )(*pieces)


def gram_of(parts):
    gram = dot(parts[0], parts[0], ((1,), (1,)))
    for part in parts[1:]:
        gram += dot(part, part, ((1,), (1,)))
    gram = gram.astype(BF)
    gram_float = gram.astype(F32)
    level = jnp.sqrt(jnp.sum(gram_float * gram_float, keepdims=True)) + norm_eps
    half = 0.5 / level
    diagonal = lax.broadcasted_iota(jnp.int32, (DIM, DIM), 0) == lax.broadcasted_iota(
        jnp.int32, (DIM, DIM), 1
    )
    first_poly = (jnp.where(diagonal, 1.5, 0.0) - gram_float * half).astype(BF)
    return gram, first_poly, half, upd_scale / jnp.sqrt(level)


def combine(rows, offset, gram, first_poly, half):
    squared = dot(rows, first_poly, ((1,), (0,))).astype(BF)
    moved = dot(squared, gram, ((1,), (0,)))
    diagonal = lax.broadcasted_iota(jnp.int32, moved.shape, 0) + offset == lax.broadcasted_iota(
        jnp.int32, moved.shape, 1
    )
    second_poly = (jnp.where(diagonal, 1.5, 0.0) - moved * half).astype(BF)
    return dot(second_poly, first_poly, ((1,), (0,))).astype(BF)


def project_kernel(scaled, weights, query_own, query_core, query_far, query_far_core, out, w, q, sem):
    x, _, c = place()
    load = pltpu.make_async_copy(weights.at[c, x // 2], w, sem)
    load.start()
    tokens = query_own.shape[0]
    q[at_place(c * tokens, tokens), :] = query_own[...]
    q[at_place((1 - c) * tokens, tokens), :] = query_core[...]
    q[at_place((2 + c) * tokens, tokens), :] = query_far[...]
    q[at_place((3 - c) * tokens, tokens), :] = query_far_core[...]
    gram, first_poly, half, factor = gram_of([scaled[...]])
    combined = combine(first_poly, 0, gram, first_poly, half)
    update = dot(combined, scaled[...], ((1,), (0,))) * factor
    load.wait()
    renewed = (w[...].astype(F32) - update).astype(BF)
    out[...] = dot(q[...], renewed, ((1,), (0,)))


def project(scaled, weights, *queries):
    tokens = queries[0].shape[0]
    return pl.pallas_call(
        project_kernel,
        out_shape=shape(4 * tokens, FF, dtype=F32),
        in_specs=[VMEM, ANY] + [VMEM] * 4,
        out_specs=VMEM,
        scratch_shapes=[
            pltpu.VMEM((DIM, FF), BF),
            pltpu.VMEM((4 * tokens, DIM), BF),
            pltpu.SemaphoreType.DMA,
        ],
        compiler_params=params(),
        cost_estimate=cost(22 * 10**8, 5 << 20),
        name="project",
    )(scaled, weights, *queries)


def third_kernel(mine, other, weights, out, scaled, w, poly, sem):
    x, _, c = place()
    rows = DIM // 2
    load = pltpu.make_async_copy(weights.at[2, x // 2, at_place(c * rows, rows)], w, sem)
    load.start()
    for side in range(2):
        cols = slice(side * QUARTER, (side + 1) * QUARTER)
        scaled[:, at_place(side * HALF + c * QUARTER, QUARTER)] = mine[:, cols]
        scaled[:, at_place(side * HALF + (1 - c) * QUARTER, QUARTER)] = other[:, cols]
    gram, first_poly, half, factor = gram_of([scaled[...]])
    poly[...] = first_poly
    combined = combine(poly[at_place(c * rows, rows), :], c * rows, gram, first_poly, half)
    update = dot(combined, scaled[...], ((1,), (0,))) * factor
    load.wait()
    out[...] = (w[...].astype(F32) - update).astype(BF)


def renew_third(mine, other, weights):
    rows = DIM // 2
    return pl.pallas_call(
        third_kernel,
        out_shape=shape(rows, FF),
        in_specs=[VMEM, VMEM, ANY],
        out_specs=VMEM,
        scratch_shapes=[
            pltpu.VMEM((DIM, FF), BF),
            pltpu.VMEM((rows, FF), BF),
            pltpu.VMEM((DIM, DIM), BF),
            pltpu.SemaphoreType.DMA,
        ],
        compiler_params=params(),
        cost_estimate=cost(12 * 10**8, 4 << 20),
        name="renew_third",
    )(mine, other, weights)


def down_kernel(mine, other, rows, own, core, far, far_core, gated, result):
    _, _, c = place()

    @pl.when(c == 0)
    def _():
        first_proj = mine[...]
        gated[...] = (first_proj * jax.nn.sigmoid(first_proj) * other[...]).astype(BF)

    @pl.when(c == 1)
    def _():
        first_proj = other[...]
        gated[...] = (first_proj * jax.nn.sigmoid(first_proj) * mine[...]).astype(BF)

    result[...] = dot(gated[...], rows[...], ((1,), (1,))).astype(BF)
    tokens = own.shape[0]
    own[...] = result[at_place(c * tokens, tokens), :]
    core[...] = result[at_place((1 - c) * tokens, tokens), :]
    far[...] = result[at_place((2 + c) * tokens, tokens), :]
    far_core[...] = result[at_place((3 - c) * tokens, tokens), :]


def down(mine, other, rows):
    tokens = mine.shape[0] // 4
    part = shape(tokens, DIM // 2)
    return pl.pallas_call(
        down_kernel,
        out_shape=(part,) * 4,
        in_specs=[VMEM] * 3,
        out_specs=(VMEM,) * 4,
        scratch_shapes=[pltpu.VMEM((4 * tokens, FF), BF), pltpu.VMEM((4 * tokens, DIM // 2), BF)],
        compiler_params=params(),
        cost_estimate=cost(3 * 10**8, 3 << 20),
        name="down",
    )(mine, other, rows)


def finish_kernel(first_out, own, core, far, far_core, out):
    x, _, c = place()
    half = DIM // 2
    here, there = x // 2 * DIM, (1 - x // 2) * DIM
    out[0] = first_out[...]
    out[1, :, at_place(here + c * half, half)] = own[...]
    out[1, :, at_place(here + (1 - c) * half, half)] = core[...]
    out[1, :, at_place(there + c * half, half)] = far[...]
    out[1, :, at_place(there + (1 - c) * half, half)] = far_core[...]


def finish(first_out, *parts):
    return pl.pallas_call(
        finish_kernel,
        out_shape=shape(2, *first_out.shape),
        in_specs=[VMEM] * 5,
        out_specs=VMEM,
        name="finish",
    )(first_out, *parts)


def body(queries, keys, values, rates, weights):
    own, far1, far2, far3, query_own, query_far = prepare(queries, keys, values, rates)
    queries_late, own = lax.optimization_barrier((queries, own))
    first_out = first_block(queries_late, weights)
    got = [own, along_x(far1, 1), along_x(far2, 2), along_x(far3, 3)]
    got += [other_core(piece) for piece in got]
    got, first_out = lax.optimization_barrier((got, first_out))
    parts = gradient(got, weights)
    query_far, parts = lax.optimization_barrier((query_far, parts))
    query_far = mirror_x(query_far)
    query_core, query_far_core = other_core(query_own), other_core(query_far)
    pieces = gather_rows(reduce_rows(parts))
    matrix, shared = pack(pieces)
    shared_core = other_core(shared)
    projected = project(matrix, weights, query_own, query_core, query_far, query_far_core)
    projected_core = other_core(projected)
    rows = renew_third(shared, shared_core, weights)
    own, core, far, far_core = down(projected, projected_core, rows)
    return finish(first_out, own, other_core(core), mirror_x(far), mirror_x_core(far_core))


def solution(mesh):
    in_specs = (
        P(None, ("dp", "ctx"), None),
        P(None, ("dp", "ctx"), None),
        P(None, ("dp", "ctx"), None),
        P(None, None, ("dp", "ctx")),
        P(),
    )
    out_specs = P(None, ("dp", "ctx"), None)
    return jax.shard_map(body, mesh=mesh, in_specs=in_specs, out_specs=out_specs, check_vma=False)
```

```python
import jax
import jax.numpy as jnp
from jax import lax
from jax.experimental import pallas as pl
from jax.experimental.pallas import tpu as pltpu
from jax.sharding import PartitionSpec as P

X, Z, C = 4, 8, 2
DIM, FF = 512, 1024
HALF, QUARTER = FF // 2, FF // 4
WIDE = HALF + QUARTER
ROWS = DIM // Z
BF, F32 = jnp.bfloat16, jnp.float32
upd_scale = 2.0
norm_eps = 1e-07
VMEM = pl.BlockSpec(memory_space=pltpu.VMEM)
ANY = pl.BlockSpec(memory_space=pl.ANY)


def place():
    index = lax.axis_index("ctx")
    return index // (Z * C), (index // C) % Z, index % C


def move(array, to):
    perm = []
    for x in range(X):
        for z in range(Z):
            for c in range(C):
                tx, tz, tc = to(x, z, c)
                perm.append(((x * Z + z) * C + c, (tx % X * Z + tz % Z) * C + tc % C))
    return lax.ppermute(array, "ctx", perm)


def along_x(array, distance):
    return move(array, lambda x, z, c: (x + distance, z, c))


def along_z(array, distance):
    return move(array, lambda x, z, c: (x, z + distance, c))


def pair_x(array):
    return move(array, lambda x, z, c: (x ^ 1, z, c))


def mirror_x(array):
    return move(array, lambda x, z, c: (X - 1 - x, z, c))


def mirror_x_core(array):
    return move(array, lambda x, z, c: (X - 1 - x, z, c + 1))


def other_core(array):
    return move(array, lambda x, z, c: (x, z, c + 1))


def dot(left, right, dims):
    return lax.dot_general(left, right, (dims, ((), ())), preferred_element_type=F32)


def shape(*dims, dtype=BF):
    return jax.ShapeDtypeStruct(dims, dtype)


def params(mib):
    return pltpu.CompilerParams(vmem_limit_bytes=mib << 20)


def cost(flops, size):
    return pl.CostEstimate(flops=flops, bytes_accessed=size, transcendentals=0)


def at_place(start, size):
    return pl.ds(pl.multiple_of(start, size), size)


def prepare_kernel(queries, keys, values, rates, own, far1, far2, far3, query_own, query_far):
    x, _, _ = place()
    tokens = keys.shape[1]
    diagonal = lax.broadcasted_iota(jnp.int32, (tokens, tokens), 0) == lax.broadcasted_iota(
        jnp.int32, (tokens, tokens), 1
    )
    for head in range(2):
        row = rates[0, head : head + 1, :]
        rate = jnp.sum(jnp.where(diagonal, row, 0.0), axis=1, keepdims=True)
        cols = slice(head * DIM, (head + 1) * DIM)
        scaled = (values[0, :, cols].astype(F32) * rate).astype(BF)
        for distance, ref in enumerate((own, far1, far2, far3)):

            @pl.when(lax.rem(x + distance, X) // 2 == head)
            def _():
                ref[:tokens, :] = keys[0, :, cols]
                ref[tokens:, :] = scaled

        @pl.when(x // 2 == head)
        def _():
            query_own[...] = queries[1, :, cols]

        @pl.when(x // 2 != head)
        def _():
            query_far[...] = queries[1, :, cols]


def prepare(queries, keys, values, rates):
    tokens = keys.shape[1]
    pair, half = shape(2 * tokens, DIM), shape(tokens, DIM)
    return pl.pallas_call(
        prepare_kernel,
        out_shape=(pair, pair, pair, pair, half, half),
        in_specs=[VMEM] * 4,
        out_specs=(VMEM,) * 6,
        compiler_params=params(3),
        name="prepare",
    )(queries, keys, values, rates)


def first_kernel(queries, weights, out, w, sem):
    copies = []
    for head in range(2):
        for m in range(3):
            copy = pltpu.make_async_copy(weights.at[m, head], w.at[head, m], sem.at[head, m])
            copy.start()
            copies.append(copy)
    for head in range(2):
        cols = slice(head * DIM, (head + 1) * DIM)
        query = queries[0, :, cols]
        copies[3 * head].wait()
        first_proj = dot(query, w[head, 0], ((1,), (0,)))
        copies[3 * head + 1].wait()
        third_proj = dot(query, w[head, 1], ((1,), (0,)))
        gated = (first_proj * jax.nn.sigmoid(first_proj) * third_proj).astype(BF)
        copies[3 * head + 2].wait()
        out[:, cols] = dot(gated, w[head, 2], ((1,), (1,))).astype(BF)


def first_block(queries, weights):
    tokens = queries.shape[1]
    return pl.pallas_call(
        first_kernel,
        out_shape=shape(tokens, 2 * DIM),
        in_specs=[VMEM, ANY],
        out_specs=VMEM,
        scratch_shapes=[pltpu.VMEM((2, 3, DIM, FF), BF), pltpu.SemaphoreType.DMA((2, 3))],
        compiler_params=params(12),
        cost_estimate=cost(12 * tokens * DIM * FF, 7 << 20),
        name="first_block",
    )(queries, weights)


def gradient_kernel(*refs):
    pieces, weights = refs[:8], refs[8]
    own, near_up, near_down, keep_up, keep_down, send_up, send_down, far_up, far_down = refs[9:18]
    w, k, v, d, gated, total, sem = refs[18:]
    x, z, c = place()
    copies = []
    for m in range(3):
        copy = pltpu.make_async_copy(
            weights.at[m, x // 2, :, at_place(lax.rem(x, 2) * HALF, HALF)], w.at[m], sem.at[m]
        )
        copy.start()
        copies.append(copy)
    tokens = pieces[0].shape[0] // 2
    for i, piece in enumerate(pieces):
        k[i * tokens : (i + 1) * tokens, :] = piece[:tokens, :]
        v[i * tokens : (i + 1) * tokens, :] = piece[tokens:, :]
    for copy in copies:
        copy.wait()
    key_first = dot(k[...], w[0], ((1,), (0,)))
    key_third = dot(k[...], w[1], ((1,), (0,)))
    back_grad = -dot(v[...], w[2], ((1,), (0,)))
    sig = jax.nn.sigmoid(key_first)
    key_act = key_first * sig

    @pl.when(c == 0)
    def _():
        d[...] = (back_grad * key_third * sig * (1.0 + key_first * (1.0 - sig))).astype(BF)
        gated[...] = (key_act[:, :QUARTER] * key_third[:, :QUARTER]).astype(BF)

    @pl.when(c == 1)
    def _():
        d[...] = (back_grad * key_act).astype(BF)
        gated[...] = (key_act[:, QUARTER:] * key_third[:, QUARTER:]).astype(BF)

    total[:, :HALF] = dot(k[...], d[...], ((0,), (0,)))
    total[:, HALF:] = -dot(v[...], gated[...], ((0,), (0,)))

    def rows(distance):
        return total[at_place(lax.rem(z + distance + Z, Z) * ROWS, ROWS), :]

    own[...] = rows(0)
    near_up[...] = rows(1).astype(BF)
    near_down[...] = rows(-1).astype(BF)
    keep_up[...] = rows(2)
    keep_down[...] = rows(-2)
    send_up[...] = rows(3).astype(BF)
    send_down[...] = rows(-3).astype(BF)
    far = rows(4).astype(BF)
    far_up[...] = far[: ROWS // 2]
    far_down[...] = far[ROWS // 2 :]


def gradient(pieces, weights):
    tokens = 8 * pieces[0].shape[0] // 2
    kept, sent, half = shape(ROWS, WIDE, dtype=F32), shape(ROWS, WIDE), shape(ROWS // 2, WIDE)
    return pl.pallas_call(
        gradient_kernel,
        out_shape=(kept, sent, sent, kept, kept, sent, sent, half, half),
        in_specs=[VMEM] * 8 + [ANY],
        out_specs=(VMEM,) * 9,
        scratch_shapes=[
            pltpu.VMEM((3, DIM, HALF), BF),
            pltpu.VMEM((tokens, DIM), BF),
            pltpu.VMEM((tokens, DIM), BF),
            pltpu.VMEM((tokens, HALF), BF),
            pltpu.VMEM((tokens, QUARTER), BF),
            pltpu.VMEM((DIM, WIDE), F32),
            pltpu.SemaphoreType.DMA((3,)),
        ],
        compiler_params=params(16),
        cost_estimate=cost(10 * tokens * DIM * HALF, 6 << 20),
        name="gradient",
    )(*pieces, weights)


def middle_kernel(keep_up, keep_down, got_up, got_down, far_up, far_down, up, down):
    half = ROWS // 2
    total = keep_up[...] + got_up[...].astype(F32)
    up[:half, :] = (total[:half] + far_up[...].astype(F32)).astype(BF)
    up[half:, :] = total[half:].astype(BF)
    total = keep_down[...] + got_down[...].astype(F32)
    down[:half, :] = total[:half].astype(BF)
    down[half:, :] = (total[half:] + far_down[...].astype(F32)).astype(BF)


def middle(*args):
    return pl.pallas_call(
        middle_kernel,
        out_shape=(shape(ROWS, WIDE), shape(ROWS, WIDE)),
        in_specs=[VMEM] * 6,
        out_specs=(VMEM, VMEM),
        compiler_params=params(3),
        name="middle",
    )(*args)


def total_kernel(own, a, b, c, d, out):
    total = own[...] + a[...].astype(F32) + b[...].astype(F32) + c[...].astype(F32)
    out[...] = (total + d[...].astype(F32)).astype(BF)


def add_up(*args):
    return pl.pallas_call(
        total_kernel,
        out_shape=shape(ROWS, WIDE),
        in_specs=[VMEM] * 5,
        out_specs=VMEM,
        compiler_params=params(3),
        name="add_up",
    )(*args)


def reduce_rows(parts):
    own, near_up, near_down, keep_up, keep_down, send_up, send_down, far_up, far_down = parts
    far_up, far_down = along_z(far_up, 2), along_z(far_down, -2)
    got_up, got_down = along_z(send_up, 1), along_z(send_down, -1)
    near_up, near_down = along_z(near_up, 1), along_z(near_down, -1)
    up, down = middle(keep_up, keep_down, got_up, got_down, far_up, far_down)
    up, down = along_z(up, 2), along_z(down, -2)
    return add_up(own, near_up, near_down, up, down)


ORIGINS = ((0, 0, ROWS), (-1, 0, ROWS), (1, 0, ROWS), (-2, 0, ROWS), (2, 0, ROWS)) + (
    (-3, 0, ROWS),
    (3, 0, ROWS),
    (-4, 0, ROWS // 2),
    (4, ROWS // 2, ROWS // 2),
)


def gather_rows(own):
    own = jnp.concatenate([own, pair_x(own)], axis=1)
    up1, down1 = along_z(own, 1), along_z(own, -1)
    up2, down2 = along_z(own, 2), along_z(own, -2)
    up3, down3 = along_z(up2, 1), along_z(down2, -1)
    up4, down4 = along_z(up2[: ROWS // 2], 2), along_z(down2[ROWS // 2 :], -2)
    return [own, up1, down1, up2, down2, up3, down3, up4, down4]


def pack_kernel(*refs):
    pieces = refs[:9]
    matrix, shared, sem = refs[9:]
    x, z, _ = place()
    copies = []
    for i, piece in enumerate(pieces):
        step, first, count = ORIGINS[i]
        rows = at_place(lax.rem(z + step + Z, Z) * ROWS + first, count)
        for j in range(4):
            side = lax.rem(x + j // 2, 2)
            target, size, offset = ((matrix, HALF, 0), (shared, QUARTER, HALF))[j % 2]
            copy = pltpu.make_async_copy(
                piece.at[:, pl.ds(j // 2 * WIDE + offset, size)],
                target.at[rows, at_place(side * size, size)],
                sem.at[i, j],
            )
            copy.start()
            copies.append(copy)
    for copy in copies:
        copy.wait()


def pack(pieces):
    return pl.pallas_call(
        pack_kernel,
        out_shape=(shape(DIM, FF), shape(DIM, HALF)),
        in_specs=[ANY] * 9,
        out_specs=(VMEM, VMEM),
        scratch_shapes=[pltpu.SemaphoreType.DMA((9, 4))],
        compiler_params=params(4),
        cost_estimate=cost(0, 3 << 20),
        name="pack",
    )(*pieces)


def gram_of(parts):
    gram = dot(parts[0], parts[0], ((1,), (1,)))
    for part in parts[1:]:
        gram += dot(part, part, ((1,), (1,)))
    gram = gram.astype(BF)
    gram_float = gram.astype(F32)
    level = jnp.sqrt(jnp.sum(gram_float * gram_float, keepdims=True)) + norm_eps
    half = 0.5 / level
    diagonal = lax.broadcasted_iota(jnp.int32, (DIM, DIM), 0) == lax.broadcasted_iota(
        jnp.int32, (DIM, DIM), 1
    )
    first_poly = (jnp.where(diagonal, 1.5, 0.0) - gram_float * half).astype(BF)
    return gram, first_poly, half, upd_scale / jnp.sqrt(level)


def combine(rows, offset, gram, first_poly, half):
    squared = dot(rows, first_poly, ((1,), (0,))).astype(BF)
    moved = dot(squared, gram, ((1,), (0,)))
    diagonal = lax.broadcasted_iota(jnp.int32, moved.shape, 0) + offset == lax.broadcasted_iota(
        jnp.int32, moved.shape, 1
    )
    second_poly = (jnp.where(diagonal, 1.5, 0.0) - moved * half).astype(BF)
    return dot(second_poly, first_poly, ((1,), (0,))).astype(BF)


def project_kernel(scaled, weights, query_own, query_core, query_far, query_far_core, out, w, q, sem):
    x, _, c = place()
    load = pltpu.make_async_copy(weights.at[c, x // 2], w, sem)
    load.start()
    tokens = query_own.shape[0]
    q[at_place(c * tokens, tokens), :] = query_own[...]
    q[at_place((1 - c) * tokens, tokens), :] = query_core[...]
    q[at_place((2 + c) * tokens, tokens), :] = query_far[...]
    q[at_place((3 - c) * tokens, tokens), :] = query_far_core[...]
    gram, first_poly, half, factor = gram_of([scaled[...]])
    combined = combine(first_poly, 0, gram, first_poly, half)
    update = dot(combined, scaled[...], ((1,), (0,))) * factor
    load.wait()
    renewed = (w[...].astype(F32) - update).astype(BF)
    out[...] = dot(q[...], renewed, ((1,), (0,)))


def project(scaled, weights, *queries):
    tokens = queries[0].shape[0]
    return pl.pallas_call(
        project_kernel,
        out_shape=shape(4 * tokens, FF, dtype=F32),
        in_specs=[VMEM, ANY] + [VMEM] * 4,
        out_specs=VMEM,
        scratch_shapes=[
            pltpu.VMEM((DIM, FF), BF),
            pltpu.VMEM((4 * tokens, DIM), BF),
            pltpu.SemaphoreType.DMA,
        ],
        compiler_params=params(16),
        cost_estimate=cost(22 * 10**8, 5 << 20),
        name="project",
    )(scaled, weights, *queries)


def third_kernel(mine, other, weights, out, scaled, w, poly, sem):
    x, _, c = place()
    rows = DIM // 2
    load = pltpu.make_async_copy(weights.at[2, x // 2, at_place(c * rows, rows)], w, sem)
    load.start()
    for side in range(2):
        cols = slice(side * QUARTER, (side + 1) * QUARTER)
        scaled[:, at_place(side * HALF + c * QUARTER, QUARTER)] = mine[:, cols]
        scaled[:, at_place(side * HALF + (1 - c) * QUARTER, QUARTER)] = other[:, cols]
    gram, first_poly, half, factor = gram_of([scaled[...]])
    poly[...] = first_poly
    combined = combine(poly[at_place(c * rows, rows), :], c * rows, gram, first_poly, half)
    update = dot(combined, scaled[...], ((1,), (0,))) * factor
    load.wait()
    out[...] = (w[...].astype(F32) - update).astype(BF)


def renew_third(mine, other, weights):
    rows = DIM // 2
    return pl.pallas_call(
        third_kernel,
        out_shape=shape(rows, FF),
        in_specs=[VMEM, VMEM, ANY],
        out_specs=VMEM,
        scratch_shapes=[
            pltpu.VMEM((DIM, FF), BF),
            pltpu.VMEM((rows, FF), BF),
            pltpu.VMEM((DIM, DIM), BF),
            pltpu.SemaphoreType.DMA,
        ],
        compiler_params=params(14),
        cost_estimate=cost(12 * 10**8, 4 << 20),
        name="renew_third",
    )(mine, other, weights)


def down_kernel(mine, other, rows, own, core, far, far_core, gated, result):
    _, _, c = place()

    @pl.when(c == 0)
    def _():
        first_proj = mine[...]
        gated[...] = (first_proj * jax.nn.sigmoid(first_proj) * other[...]).astype(BF)

    @pl.when(c == 1)
    def _():
        first_proj = other[...]
        gated[...] = (first_proj * jax.nn.sigmoid(first_proj) * mine[...]).astype(BF)

    result[...] = dot(gated[...], rows[...], ((1,), (1,))).astype(BF)
    tokens = own.shape[0]
    own[...] = result[at_place(c * tokens, tokens), :]
    core[...] = result[at_place((1 - c) * tokens, tokens), :]
    far[...] = result[at_place((2 + c) * tokens, tokens), :]
    far_core[...] = result[at_place((3 - c) * tokens, tokens), :]


def down(mine, other, rows):
    tokens = mine.shape[0] // 4
    part = shape(tokens, DIM // 2)
    return pl.pallas_call(
        down_kernel,
        out_shape=(part,) * 4,
        in_specs=[VMEM] * 3,
        out_specs=(VMEM,) * 4,
        scratch_shapes=[pltpu.VMEM((4 * tokens, FF), BF), pltpu.VMEM((4 * tokens, DIM // 2), BF)],
        compiler_params=params(8),
        cost_estimate=cost(3 * 10**8, 3 << 20),
        name="down",
    )(mine, other, rows)


def finish_kernel(first_out, own, core, far, far_core, out):
    x, _, c = place()
    half = DIM // 2
    here, there = x // 2 * DIM, (1 - x // 2) * DIM
    out[0] = first_out[...]
    out[1, :, at_place(here + c * half, half)] = own[...]
    out[1, :, at_place(here + (1 - c) * half, half)] = core[...]
    out[1, :, at_place(there + c * half, half)] = far[...]
    out[1, :, at_place(there + (1 - c) * half, half)] = far_core[...]


def finish(first_out, *parts):
    return pl.pallas_call(
        finish_kernel,
        out_shape=shape(2, *first_out.shape),
        in_specs=[VMEM] * 5,
        out_specs=VMEM,
        compiler_params=params(2),
        name="finish",
    )(first_out, *parts)


def body(queries, keys, values, rates, weights):
    own, far1, far2, far3, query_own, query_far = prepare(queries, keys, values, rates)
    queries_late, own = lax.optimization_barrier((queries, own))
    first_out = first_block(queries_late, weights)
    got = [own, along_x(far1, 1), along_x(far2, 2), along_x(far3, 3)]
    got, first_out = lax.optimization_barrier((got, first_out))
    got += [other_core(piece) for piece in got]
    parts = gradient(got, weights)
    query_far, parts = lax.optimization_barrier((query_far, parts))
    query_far = mirror_x(query_far)
    query_core, query_far_core = other_core(query_own), other_core(query_far)
    pieces = gather_rows(reduce_rows(parts))
    matrix, shared = pack(pieces)
    shared_core = other_core(shared)
    projected = project(matrix, weights, query_own, query_core, query_far, query_far_core)
    projected, shared_core = lax.optimization_barrier((projected, shared_core))
    projected_core = other_core(projected)
    rows = renew_third(shared, shared_core, weights)
    own, core, far, far_core = down(projected, projected_core, rows)
    return finish(first_out, own, other_core(core), mirror_x(far), mirror_x_core(far_core))


def solution(mesh):
    in_specs = (
        P(None, ("dp", "ctx"), None),
        P(None, ("dp", "ctx"), None),
        P(None, ("dp", "ctx"), None),
        P(None, None, ("dp", "ctx")),
        P(),
    )
    out_specs = P(None, ("dp", "ctx"), None)
    return jax.shard_map(body, mesh=mesh, in_specs=in_specs, out_specs=out_specs, check_vma=False)
```

```python
import jax
import jax.numpy as jnp
from jax import lax
from jax.experimental import pallas as pl
from jax.experimental.pallas import tpu as pltpu
from jax.sharding import PartitionSpec as P

X, Z, C = 4, 8, 2
DIM, FF = 512, 1024
HALF, QUARTER = FF // 2, FF // 4
WIDE = HALF + QUARTER
ROWS = DIM // Z
BF, F32 = jnp.bfloat16, jnp.float32
upd_scale = 2.0
norm_eps = 1e-07
VMEM = pl.BlockSpec(memory_space=pltpu.VMEM)
ANY = pl.BlockSpec(memory_space=pl.ANY)
HBM = pl.BlockSpec(memory_space=pltpu.HBM)


def place():
    index = lax.axis_index("ctx")
    return index // (Z * C), (index // C) % Z, index % C


def move(array, to):
    perm = []
    for x in range(X):
        for z in range(Z):
            for c in range(C):
                tx, tz, tc = to(x, z, c)
                perm.append(((x * Z + z) * C + c, (tx % X * Z + tz % Z) * C + tc % C))
    return lax.ppermute(array, "ctx", perm)


def along_x(array, distance):
    return move(array, lambda x, z, c: (x + distance, z, c))


def along_z(array, distance):
    return move(array, lambda x, z, c: (x, z + distance, c))


def pair_x(array):
    return move(array, lambda x, z, c: (x ^ 1, z, c))


def mirror_x(array):
    return move(array, lambda x, z, c: (X - 1 - x, z, c))


def mirror_x_core(array):
    return move(array, lambda x, z, c: (X - 1 - x, z, c + 1))


def other_core(array):
    return move(array, lambda x, z, c: (x, z, c + 1))


def dot(left, right, dims):
    return lax.dot_general(left, right, (dims, ((), ())), preferred_element_type=F32)


def shape(*dims, dtype=BF):
    return jax.ShapeDtypeStruct(dims, dtype)


def params(mib):
    return pltpu.CompilerParams(vmem_limit_bytes=mib << 20)


def cost(flops, size):
    return pl.CostEstimate(flops=flops, bytes_accessed=size, transcendentals=0)


def at_place(start, size):
    return pl.ds(pl.multiple_of(start, size), size)


def prepare_kernel(queries, keys, values, rates, *refs):
    own, far1, far2, far3, query_own, query_far, q, k, v, r, sem = refs
    copies = []
    for i, (source, target) in enumerate(
        ((rates, r), (values.at[0], v), (keys.at[0], k), (queries.at[1], q))
    ):
        copy = pltpu.make_async_copy(source, target, sem.at[i])
        copy.start()
        copies.append(copy)
    x, _, _ = place()
    tokens = k.shape[0]
    diagonal = lax.broadcasted_iota(jnp.int32, (tokens, tokens), 0) == lax.broadcasted_iota(
        jnp.int32, (tokens, tokens), 1
    )
    for copy in copies:
        copy.wait()
    for head in range(2):
        row = r[0, head : head + 1, :]
        rate = jnp.sum(jnp.where(diagonal, row, 0.0), axis=1, keepdims=True)
        cols = slice(head * DIM, (head + 1) * DIM)
        scaled = (v[:, cols].astype(F32) * rate).astype(BF)
        for distance, ref in enumerate((own, far1, far2, far3)):

            @pl.when(lax.rem(x + distance, X) // 2 == head)
            def _():
                ref[:tokens, :] = k[:, cols]
                ref[tokens:, :] = scaled

        @pl.when(x // 2 == head)
        def _():
            query_own[...] = q[:, cols]

        @pl.when(x // 2 != head)
        def _():
            query_far[...] = q[:, cols]


def prepare(queries, keys, values, rates):
    tokens = keys.shape[1]
    pair, half = shape(2 * tokens, DIM), shape(tokens, DIM)
    wide = pltpu.VMEM((tokens, 2 * DIM), BF)
    return pl.pallas_call(
        prepare_kernel,
        out_shape=(pair, pair, pair, pair, half, half),
        in_specs=[HBM] * 4,
        out_specs=(VMEM,) * 6,
        scratch_shapes=[
            wide,
            wide,
            wide,
            pltpu.VMEM(rates.shape, F32),
            pltpu.SemaphoreType.DMA((4,)),
        ],
        name="prepare",
    )(queries, keys, values, rates)


def first_kernel(queries, weights, out, q, w, sem, query_sem):
    load_query = pltpu.make_async_copy(queries.at[0], q, query_sem)
    load_query.start()
    copies = []
    for head in range(2):
        for m in range(3):
            copy = pltpu.make_async_copy(weights.at[m, head], w.at[head, m], sem.at[head, m])
            copy.start()
            copies.append(copy)
    load_query.wait()
    for head in range(2):
        cols = slice(head * DIM, (head + 1) * DIM)
        query = q[:, cols]
        copies[3 * head].wait()
        first_proj = dot(query, w[head, 0], ((1,), (0,)))
        copies[3 * head + 1].wait()
        third_proj = dot(query, w[head, 1], ((1,), (0,)))
        gated = (first_proj * jax.nn.sigmoid(first_proj) * third_proj).astype(BF)
        copies[3 * head + 2].wait()
        out[:, cols] = dot(gated, w[head, 2], ((1,), (1,))).astype(BF)


def first_block(queries, weights):
    tokens = queries.shape[1]
    return pl.pallas_call(
        first_kernel,
        out_shape=shape(tokens, 2 * DIM),
        in_specs=[HBM, HBM],
        out_specs=VMEM,
        scratch_shapes=[
            pltpu.VMEM((tokens, 2 * DIM), BF),
            pltpu.VMEM((2, 3, DIM, FF), BF),
            pltpu.SemaphoreType.DMA((2, 3)),
            pltpu.SemaphoreType.DMA,
        ],
        compiler_params=params(12),
        cost_estimate=cost(12 * tokens * DIM * FF, 7 << 20),
        name="first_block",
    )(queries, weights)


def load_kernel(weights, out, sem):
    x, _, _ = place()
    copies = []
    for m in range(3):
        copy = pltpu.make_async_copy(
            weights.at[m, x // 2, :, at_place(lax.rem(x, 2) * HALF, HALF)], out.at[m], sem.at[m]
        )
        copy.start()
        copies.append(copy)
    for copy in copies:
        copy.wait()


def load(weights):
    return pl.pallas_call(
        load_kernel,
        out_shape=shape(3, DIM, HALF),
        in_specs=[HBM],
        out_specs=VMEM,
        scratch_shapes=[pltpu.SemaphoreType.DMA((3,))],
        compiler_params=params(2),
        cost_estimate=cost(0, 3 << 20),
        name="load",
    )(weights)


def gradient_kernel(*refs):
    pieces, w = refs[:8], refs[8]
    own, near_up, near_down, keep_up, keep_down, send_up, send_down, far_up, far_down = refs[9:18]
    k, v, d, gated, total = refs[18:]
    _, z, c = place()
    tokens = pieces[0].shape[0] // 2
    for i, piece in enumerate(pieces):
        k[i * tokens : (i + 1) * tokens, :] = piece[:tokens, :]
        v[i * tokens : (i + 1) * tokens, :] = piece[tokens:, :]
    key_first = dot(k[...], w[0], ((1,), (0,)))
    key_third = dot(k[...], w[1], ((1,), (0,)))
    back_grad = -dot(v[...], w[2], ((1,), (0,)))
    sig = jax.nn.sigmoid(key_first)
    key_act = key_first * sig

    @pl.when(c == 0)
    def _():
        d[...] = (back_grad * key_third * sig * (1.0 + key_first * (1.0 - sig))).astype(BF)
        gated[...] = (key_act[:, :QUARTER] * key_third[:, :QUARTER]).astype(BF)

    @pl.when(c == 1)
    def _():
        d[...] = (back_grad * key_act).astype(BF)
        gated[...] = (key_act[:, QUARTER:] * key_third[:, QUARTER:]).astype(BF)

    total[:, :HALF] = dot(k[...], d[...], ((0,), (0,)))
    total[:, HALF:] = -dot(v[...], gated[...], ((0,), (0,)))

    def rows(distance):
        return total[at_place(lax.rem(z + distance + Z, Z) * ROWS, ROWS), :]

    own[...] = rows(0)
    near_up[...] = rows(1).astype(BF)
    near_down[...] = rows(-1).astype(BF)
    keep_up[...] = rows(2)
    keep_down[...] = rows(-2)
    send_up[...] = rows(3).astype(BF)
    send_down[...] = rows(-3).astype(BF)
    far = rows(4).astype(BF)
    far_up[...] = far[: ROWS // 2]
    far_down[...] = far[ROWS // 2 :]


def gradient(pieces, weights):
    tokens = 8 * pieces[0].shape[0] // 2
    kept, sent, half = shape(ROWS, WIDE, dtype=F32), shape(ROWS, WIDE), shape(ROWS // 2, WIDE)
    return pl.pallas_call(
        gradient_kernel,
        out_shape=(kept, sent, sent, kept, kept, sent, sent, half, half),
        in_specs=[VMEM] * 9,
        out_specs=(VMEM,) * 9,
        scratch_shapes=[
            pltpu.VMEM((tokens, DIM), BF),
            pltpu.VMEM((tokens, DIM), BF),
            pltpu.VMEM((tokens, HALF), BF),
            pltpu.VMEM((tokens, QUARTER), BF),
            pltpu.VMEM((DIM, WIDE), F32),
        ],
        compiler_params=params(16),
        cost_estimate=cost(10 * tokens * DIM * HALF, 6 << 20),
        name="gradient",
    )(*pieces, weights)


def middle_kernel(keep_up, keep_down, got_up, got_down, far_up, far_down, up, down):
    half = ROWS // 2
    total = keep_up[...] + got_up[...].astype(F32)
    up[:half, :] = (total[:half] + far_up[...].astype(F32)).astype(BF)
    up[half:, :] = total[half:].astype(BF)
    total = keep_down[...] + got_down[...].astype(F32)
    down[:half, :] = total[:half].astype(BF)
    down[half:, :] = (total[half:] + far_down[...].astype(F32)).astype(BF)


def middle(*args):
    return pl.pallas_call(
        middle_kernel,
        out_shape=(shape(ROWS, WIDE), shape(ROWS, WIDE)),
        in_specs=[VMEM] * 6,
        out_specs=(VMEM, VMEM),
        compiler_params=params(3),
        name="middle",
    )(*args)


def total_kernel(own, a, b, c, d, out):
    total = own[...] + a[...].astype(F32) + b[...].astype(F32) + c[...].astype(F32)
    out[...] = (total + d[...].astype(F32)).astype(BF)


def add_up(*args):
    return pl.pallas_call(
        total_kernel,
        out_shape=shape(ROWS, WIDE),
        in_specs=[VMEM] * 5,
        out_specs=VMEM,
        compiler_params=params(3),
        name="add_up",
    )(*args)


def reduce_rows(parts):
    own, near_up, near_down, keep_up, keep_down, send_up, send_down, far_up, far_down = parts
    far_up, far_down = along_z(far_up, 2), along_z(far_down, -2)
    got_up, got_down = along_z(send_up, 1), along_z(send_down, -1)
    near_up, near_down = along_z(near_up, 1), along_z(near_down, -1)
    up, down = middle(keep_up, keep_down, got_up, got_down, far_up, far_down)
    up, down = along_z(up, 2), along_z(down, -2)
    return add_up(own, near_up, near_down, up, down)


ORIGINS = ((0, 0, ROWS), (-1, 0, ROWS), (1, 0, ROWS), (-2, 0, ROWS), (2, 0, ROWS)) + (
    (-3, 0, ROWS),
    (3, 0, ROWS),
    (-4, 0, ROWS // 2),
    (4, ROWS // 2, ROWS // 2),
)


def gather_rows(own):
    up1, down1 = along_z(own, 1), along_z(own, -1)
    up2, down2 = along_z(own, 2), along_z(own, -2)
    up3, down3 = along_z(up2, 1), along_z(down2, -1)
    up4, down4 = along_z(up2[: ROWS // 2], 2), along_z(down2[ROWS // 2 :], -2)
    return [own, up1, down1, up2, down2, up3, down3, up4, down4]


def pack_kernel(*refs):
    pieces = refs[:9]
    matrix, shared, sem = refs[9:]
    x, z, _ = place()
    copies = []
    for i, piece in enumerate(pieces):
        step, first, count = ORIGINS[i]
        rows = at_place(lax.rem(z + step + Z, Z) * ROWS + first, count)
        for j in range(4):
            side = lax.rem(x + j // 2, 2)
            target, size, offset = ((matrix, HALF, 0), (shared, QUARTER, HALF))[j % 2]
            copy = pltpu.make_async_copy(
                piece.at[:, pl.ds(j // 2 * WIDE + offset, size)],
                target.at[rows, at_place(side * size, size)],
                sem.at[i, j],
            )
            copy.start()
            copies.append(copy)
    for copy in copies:
        copy.wait()


def pack(pieces):
    return pl.pallas_call(
        pack_kernel,
        out_shape=(shape(DIM, FF), shape(DIM, HALF)),
        in_specs=[ANY] * 9,
        out_specs=(VMEM, VMEM),
        scratch_shapes=[pltpu.SemaphoreType.DMA((9, 4))],
        compiler_params=params(4),
        cost_estimate=cost(0, 3 << 20),
        name="pack",
    )(*pieces)


def gram_of(parts):
    gram = dot(parts[0], parts[0], ((1,), (1,)))
    for part in parts[1:]:
        gram += dot(part, part, ((1,), (1,)))
    gram = gram.astype(BF)
    gram_float = gram.astype(F32)
    level = jnp.sqrt(jnp.sum(gram_float * gram_float, keepdims=True)) + norm_eps
    half = 0.5 / level
    diagonal = lax.broadcasted_iota(jnp.int32, (DIM, DIM), 0) == lax.broadcasted_iota(
        jnp.int32, (DIM, DIM), 1
    )
    first_poly = (jnp.where(diagonal, 1.5, 0.0) - gram_float * half).astype(BF)
    return gram, first_poly, half, upd_scale / jnp.sqrt(level)


def combine(rows, offset, gram, first_poly, half):
    squared = dot(rows, first_poly, ((1,), (0,))).astype(BF)
    moved = dot(squared, gram, ((1,), (0,)))
    diagonal = lax.broadcasted_iota(jnp.int32, moved.shape, 0) + offset == lax.broadcasted_iota(
        jnp.int32, moved.shape, 1
    )
    second_poly = (jnp.where(diagonal, 1.5, 0.0) - moved * half).astype(BF)
    return dot(second_poly, first_poly, ((1,), (0,))).astype(BF)


def project_kernel(scaled, weights, query_own, query_core, query_far, query_far_core, out, w, q, sem):
    x, _, c = place()
    load = pltpu.make_async_copy(weights.at[c, x // 2], w, sem)
    load.start()
    tokens = query_own.shape[0]
    q[at_place(c * tokens, tokens), :] = query_own[...]
    q[at_place((1 - c) * tokens, tokens), :] = query_core[...]
    q[at_place((2 + c) * tokens, tokens), :] = query_far[...]
    q[at_place((3 - c) * tokens, tokens), :] = query_far_core[...]
    gram, first_poly, half, factor = gram_of([scaled[...]])
    combined = combine(first_poly, 0, gram, first_poly, half)
    update = dot(combined, scaled[...], ((1,), (0,))) * factor
    load.wait()
    renewed = (w[...].astype(F32) - update).astype(BF)
    out[...] = dot(q[...], renewed, ((1,), (0,)))


def project(scaled, weights, *queries):
    tokens = queries[0].shape[0]
    return pl.pallas_call(
        project_kernel,
        out_shape=shape(4 * tokens, FF, dtype=F32),
        in_specs=[VMEM, HBM] + [VMEM] * 4,
        out_specs=VMEM,
        scratch_shapes=[
            pltpu.VMEM((DIM, FF), BF),
            pltpu.VMEM((4 * tokens, DIM), BF),
            pltpu.SemaphoreType.DMA,
        ],
        compiler_params=params(16),
        cost_estimate=cost(22 * 10**8, 5 << 20),
        name="project",
    )(scaled, weights, *queries)


def third_kernel(mine, other, weights, out, scaled, w, poly, sem):
    x, _, c = place()
    rows = DIM // 2
    load = pltpu.make_async_copy(weights.at[2, x // 2, at_place(c * rows, rows)], w, sem)
    load.start()
    for side in range(2):
        cols = slice(side * QUARTER, (side + 1) * QUARTER)
        scaled[:, at_place(side * HALF + c * QUARTER, QUARTER)] = mine[:, cols]
        scaled[:, at_place(side * HALF + (1 - c) * QUARTER, QUARTER)] = other[:, cols]
    gram, first_poly, half, factor = gram_of([scaled[...]])
    poly[...] = first_poly
    combined = combine(poly[at_place(c * rows, rows), :], c * rows, gram, first_poly, half)
    update = dot(combined, scaled[...], ((1,), (0,))) * factor
    load.wait()
    out[...] = (w[...].astype(F32) - update).astype(BF)


def renew_third(mine, other, weights):
    rows = DIM // 2
    return pl.pallas_call(
        third_kernel,
        out_shape=shape(rows, FF),
        in_specs=[VMEM, VMEM, HBM],
        out_specs=VMEM,
        scratch_shapes=[
            pltpu.VMEM((DIM, FF), BF),
            pltpu.VMEM((rows, FF), BF),
            pltpu.VMEM((DIM, DIM), BF),
            pltpu.SemaphoreType.DMA,
        ],
        compiler_params=params(14),
        cost_estimate=cost(12 * 10**8, 4 << 20),
        name="renew_third",
    )(mine, other, weights)


def down_kernel(mine, other, rows, own, core, far, far_core, gated, result):
    _, _, c = place()

    @pl.when(c == 0)
    def _():
        first_proj = mine[...]
        gated[...] = (first_proj * jax.nn.sigmoid(first_proj) * other[...]).astype(BF)

    @pl.when(c == 1)
    def _():
        first_proj = other[...]
        gated[...] = (first_proj * jax.nn.sigmoid(first_proj) * mine[...]).astype(BF)

    result[...] = dot(gated[...], rows[...], ((1,), (1,))).astype(BF)
    tokens = own.shape[0]
    own[...] = result[at_place(c * tokens, tokens), :]
    core[...] = result[at_place((1 - c) * tokens, tokens), :]
    far[...] = result[at_place((2 + c) * tokens, tokens), :]
    far_core[...] = result[at_place((3 - c) * tokens, tokens), :]


def down(mine, other, rows):
    tokens = mine.shape[0] // 4
    part = shape(tokens, DIM // 2)
    return pl.pallas_call(
        down_kernel,
        out_shape=(part,) * 4,
        in_specs=[VMEM] * 3,
        out_specs=(VMEM,) * 4,
        scratch_shapes=[pltpu.VMEM((4 * tokens, FF), BF), pltpu.VMEM((4 * tokens, DIM // 2), BF)],
        compiler_params=params(8),
        cost_estimate=cost(3 * 10**8, 3 << 20),
        name="down",
    )(mine, other, rows)


def finish_kernel(first_out, own, core, far, far_core, out):
    x, _, c = place()
    half = DIM // 2
    here, there = x // 2 * DIM, (1 - x // 2) * DIM
    out[0] = first_out[...]
    out[1, :, at_place(here + c * half, half)] = own[...]
    out[1, :, at_place(here + (1 - c) * half, half)] = core[...]
    out[1, :, at_place(there + c * half, half)] = far[...]
    out[1, :, at_place(there + (1 - c) * half, half)] = far_core[...]


def finish(first_out, *parts):
    return pl.pallas_call(
        finish_kernel,
        out_shape=shape(2, *first_out.shape),
        in_specs=[VMEM] * 5,
        out_specs=VMEM,
        compiler_params=params(2),
        name="finish",
    )(first_out, *parts)


def body(queries, keys, values, rates, weights):
    barrier = lax.optimization_barrier
    own, far1, far2, far3, query_own, query_far = prepare(queries, keys, values, rates)
    own, weights = barrier((own, weights))
    got = [own, along_x(far1, 1), along_x(far2, 2), along_x(far3, 3)]
    got, query_far, part = barrier((got, query_far, load(weights)))
    query_far = mirror_x(query_far)
    got += [other_core(piece) for piece in got]
    parts, query_far = barrier((gradient(got, part), query_far))
    own, queries, query_own, query_far = barrier(
        (reduce_rows(parts), queries, query_own, query_far)
    )
    first_out = first_block(queries, weights)
    query_core, query_far_core = other_core(query_own), other_core(query_far)
    own, near, first_out, query_core, query_far_core = barrier(
        (own, pair_x(own), first_out, query_core, query_far_core)
    )
    pieces = gather_rows(jnp.concatenate([own, near], axis=1))
    matrix, shared = pack(pieces)
    shared_core = other_core(shared)
    projected = project(matrix, weights, query_own, query_core, query_far, query_far_core)
    projected, shared_core = lax.optimization_barrier((projected, shared_core))
    projected_core = other_core(projected)
    rows = renew_third(shared, shared_core, weights)
    own, core, far, far_core = down(projected, projected_core, rows)
    return finish(first_out, own, other_core(core), mirror_x(far), mirror_x_core(far_core))


def solution(mesh):
    in_specs = (
        P(None, ("dp", "ctx"), None),
        P(None, ("dp", "ctx"), None),
        P(None, ("dp", "ctx"), None),
        P(None, None, ("dp", "ctx")),
        P(),
    )
    out_specs = P(None, ("dp", "ctx"), None)
    return jax.shard_map(body, mesh=mesh, in_specs=in_specs, out_specs=out_specs, check_vma=False)
```

```python
import jax
import jax.numpy as jnp
from jax import lax
from jax.experimental import pallas as pl
from jax.experimental.pallas import tpu as pltpu
from jax.sharding import PartitionSpec as P

X, Z, C = 4, 8, 2
DIM, FF = 512, 1024
HALF, QUARTER = FF // 2, FF // 4
WIDE = HALF + QUARTER
ROWS = DIM // Z
BF, F32 = jnp.bfloat16, jnp.float32
upd_scale = 2.0
norm_eps = 1e-07
VMEM = pl.BlockSpec(memory_space=pltpu.VMEM)
ANY = pl.BlockSpec(memory_space=pl.ANY)
HBM = pl.BlockSpec(memory_space=pltpu.HBM)


barrier = lax.optimization_barrier


def place():
    index = lax.axis_index("ctx")
    return index // (Z * C), (index // C) % Z, index % C


def move(array, to):
    perm = []
    for x in range(X):
        for z in range(Z):
            for c in range(C):
                tx, tz, tc = to(x, z, c)
                perm.append(((x * Z + z) * C + c, (tx % X * Z + tz % Z) * C + tc % C))
    return lax.ppermute(array, "ctx", perm)


def along_x(array, distance):
    return move(array, lambda x, z, c: (x + distance, z, c))


def along_z(array, distance):
    return move(array, lambda x, z, c: (x, z + distance, c))


def pair_x(array):
    return move(array, lambda x, z, c: (x ^ 1, z, c))


def mirror_x(array):
    return move(array, lambda x, z, c: (X - 1 - x, z, c))


def mirror_x_core(array):
    return move(array, lambda x, z, c: (X - 1 - x, z, c + 1))


def other_core(array):
    return move(array, lambda x, z, c: (x, z, c + 1))


def dot(left, right, dims):
    return lax.dot_general(left, right, (dims, ((), ())), preferred_element_type=F32)


def shape(*dims, dtype=BF):
    return jax.ShapeDtypeStruct(dims, dtype)


def params(mib):
    return pltpu.CompilerParams(vmem_limit_bytes=mib << 20)


def cost(flops, size):
    return pl.CostEstimate(flops=flops, bytes_accessed=size, transcendentals=0)


def at_place(start, size):
    return pl.ds(pl.multiple_of(start, size), size)


def prepare_kernel(queries, keys, values, rates, *refs):
    own, far1, far2, far3, query_own, query_far, q, k, v, r, sem = refs
    copies = []
    for i, (source, target) in enumerate(
        ((rates, r), (values.at[0], v), (keys.at[0], k), (queries.at[1], q))
    ):
        copy = pltpu.make_async_copy(source, target, sem.at[i])
        copy.start()
        copies.append(copy)
    x, _, _ = place()
    tokens = k.shape[0]
    diagonal = lax.broadcasted_iota(jnp.int32, (tokens, tokens), 0) == lax.broadcasted_iota(
        jnp.int32, (tokens, tokens), 1
    )
    for copy in copies:
        copy.wait()
    for head in range(2):
        row = r[0, head : head + 1, :]
        rate = jnp.sum(jnp.where(diagonal, row, 0.0), axis=1, keepdims=True)
        cols = slice(head * DIM, (head + 1) * DIM)
        scaled = (v[:, cols].astype(F32) * rate).astype(BF)
        for distance, ref in enumerate((own, far1, far2, far3)):

            @pl.when(lax.rem(x + distance, X) // 2 == head)
            def _():
                ref[:tokens, :] = k[:, cols]
                ref[tokens:, :] = scaled

        @pl.when(x // 2 == head)
        def _():
            query_own[...] = q[:, cols]

        @pl.when(x // 2 != head)
        def _():
            query_far[...] = q[:, cols]


def prepare(queries, keys, values, rates):
    tokens = keys.shape[1]
    pair, half = shape(2 * tokens, DIM), shape(tokens, DIM)
    wide = pltpu.VMEM((tokens, 2 * DIM), BF)
    return pl.pallas_call(
        prepare_kernel,
        out_shape=(pair, pair, pair, pair, half, half),
        in_specs=[HBM] * 4,
        out_specs=(VMEM,) * 6,
        scratch_shapes=[
            wide,
            wide,
            wide,
            pltpu.VMEM(rates.shape, F32),
            pltpu.SemaphoreType.DMA((4,)),
        ],
        name="prepare",
    )(queries, keys, values, rates)


def first_kernel(queries, weights, out, q, w, sem, query_sem):
    load_query = pltpu.make_async_copy(queries.at[0], q, query_sem)
    load_query.start()
    copies = []
    for head in range(2):
        for m in range(3):
            copy = pltpu.make_async_copy(weights.at[m, head], w.at[head, m], sem.at[head, m])
            copy.start()
            copies.append(copy)
    load_query.wait()
    for head in range(2):
        cols = slice(head * DIM, (head + 1) * DIM)
        query = q[:, cols]
        copies[3 * head].wait()
        first_proj = dot(query, w[head, 0], ((1,), (0,)))
        copies[3 * head + 1].wait()
        third_proj = dot(query, w[head, 1], ((1,), (0,)))
        gated = (first_proj * jax.nn.sigmoid(first_proj) * third_proj).astype(BF)
        copies[3 * head + 2].wait()
        out[:, cols] = dot(gated, w[head, 2], ((1,), (1,))).astype(BF)


def first_block(queries, weights):
    tokens = queries.shape[1]
    return pl.pallas_call(
        first_kernel,
        out_shape=shape(tokens, 2 * DIM),
        in_specs=[HBM, HBM],
        out_specs=VMEM,
        scratch_shapes=[
            pltpu.VMEM((tokens, 2 * DIM), BF),
            pltpu.VMEM((2, 3, DIM, FF), BF),
            pltpu.SemaphoreType.DMA((2, 3)),
            pltpu.SemaphoreType.DMA,
        ],
        compiler_params=params(12),
        cost_estimate=cost(12 * tokens * DIM * FF, 7 << 20),
        name="first_block",
    )(queries, weights)


def load_kernel(weights, out, sem):
    x, _, _ = place()
    copies = []
    for m in range(3):
        copy = pltpu.make_async_copy(
            weights.at[m, x // 2, :, at_place(lax.rem(x, 2) * HALF, HALF)], out.at[m], sem.at[m]
        )
        copy.start()
        copies.append(copy)
    for copy in copies:
        copy.wait()


def load(weights):
    return pl.pallas_call(
        load_kernel,
        out_shape=shape(3, DIM, HALF),
        in_specs=[HBM],
        out_specs=VMEM,
        scratch_shapes=[pltpu.SemaphoreType.DMA((3,))],
        compiler_params=params(2),
        cost_estimate=cost(0, 3 << 20),
        name="load",
    )(weights)


def gradient_kernel(*refs):
    pieces, w = refs[:8], refs[8]
    own, up, down, keep_up, keep_down, far_up, far_down = refs[9:16]
    k, v, d, gated, total = refs[16:]
    _, z, c = place()
    tokens = pieces[0].shape[0] // 2
    for i, piece in enumerate(pieces):
        k[i * tokens : (i + 1) * tokens, :] = piece[:tokens, :]
        v[i * tokens : (i + 1) * tokens, :] = piece[tokens:, :]
    key_first = dot(k[...], w[0], ((1,), (0,)))
    key_third = dot(k[...], w[1], ((1,), (0,)))
    back_grad = -dot(v[...], w[2], ((1,), (0,)))
    sig = jax.nn.sigmoid(key_first)
    key_act = key_first * sig

    @pl.when(c == 0)
    def _():
        d[...] = (back_grad * key_third * sig * (1.0 + key_first * (1.0 - sig))).astype(BF)
        gated[...] = (key_act[:, :QUARTER] * key_third[:, :QUARTER]).astype(BF)

    @pl.when(c == 1)
    def _():
        d[...] = (back_grad * key_act).astype(BF)
        gated[...] = (key_act[:, QUARTER:] * key_third[:, QUARTER:]).astype(BF)

    total[:, :HALF] = dot(k[...], d[...], ((0,), (0,)))
    total[:, HALF:] = -dot(v[...], gated[...], ((0,), (0,)))

    def rows(distance):
        return total[at_place(lax.rem(z + distance + Z, Z) * ROWS, ROWS), :]

    own[...] = rows(0)
    up[:ROWS, :] = rows(1).astype(BF)
    up[ROWS:, :] = rows(3).astype(BF)
    down[:ROWS, :] = rows(-1).astype(BF)
    down[ROWS:, :] = rows(-3).astype(BF)
    keep_up[...] = rows(2)
    keep_down[...] = rows(-2)
    far = rows(4).astype(BF)
    far_up[...] = far[: ROWS // 2]
    far_down[...] = far[ROWS // 2 :]


def gradient(pieces, weights):
    tokens = 8 * pieces[0].shape[0] // 2
    kept, sent, half = shape(ROWS, WIDE, dtype=F32), shape(2 * ROWS, WIDE), shape(ROWS // 2, WIDE)
    return pl.pallas_call(
        gradient_kernel,
        out_shape=(kept, sent, sent, kept, kept, half, half),
        in_specs=[VMEM] * 9,
        out_specs=(VMEM,) * 7,
        scratch_shapes=[
            pltpu.VMEM((tokens, DIM), BF),
            pltpu.VMEM((tokens, DIM), BF),
            pltpu.VMEM((tokens, HALF), BF),
            pltpu.VMEM((tokens, QUARTER), BF),
            pltpu.VMEM((DIM, WIDE), F32),
        ],
        compiler_params=params(16),
        cost_estimate=cost(10 * tokens * DIM * HALF, 6 << 20),
        name="gradient",
    )(*pieces, weights)


def middle_kernel(keep_up, keep_down, got_up, got_down, far_up, far_down, up, down):
    half = ROWS // 2
    total = keep_up[...] + got_up[ROWS:, :].astype(F32)
    up[:half, :] = (total[:half] + far_up[...].astype(F32)).astype(BF)
    up[half:, :] = total[half:].astype(BF)
    total = keep_down[...] + got_down[ROWS:, :].astype(F32)
    down[:half, :] = total[:half].astype(BF)
    down[half:, :] = (total[half:] + far_down[...].astype(F32)).astype(BF)


def middle(*args):
    return pl.pallas_call(
        middle_kernel,
        out_shape=(shape(ROWS, WIDE), shape(ROWS, WIDE)),
        in_specs=[VMEM] * 6,
        out_specs=(VMEM, VMEM),
        compiler_params=params(3),
        name="middle",
    )(*args)


def total_kernel(own, a, b, c, d, out):
    total = own[...] + a[:ROWS, :].astype(F32) + b[:ROWS, :].astype(F32) + c[...].astype(F32)
    out[...] = (total + d[...].astype(F32)).astype(BF)


def add_up(*args):
    return pl.pallas_call(
        total_kernel,
        out_shape=shape(ROWS, WIDE),
        in_specs=[VMEM] * 5,
        out_specs=VMEM,
        compiler_params=params(3),
        name="add_up",
    )(*args)


def reduce_rows(parts, query_own, query_far):
    own, up, down, keep_up, keep_down, far_up, far_down = parts
    far_up, far_down = along_z(far_up, 2), along_z(far_down, -2)
    got_up, got_down = along_z(up, 1), along_z(down, -1)
    up, down = middle(keep_up, keep_down, got_up, got_down, far_up, far_down)
    up, down, query_own, query_far = barrier((up, down, query_own, query_far))
    up, down = along_z(up, 2), along_z(down, -2)
    up, down, query_core, query_far_core = barrier(
        (up, down, other_core(query_own), other_core(query_far))
    )
    return add_up(own, got_up, got_down, up, down), (query_own, query_core, query_far, query_far_core)


ORIGINS = ((0, 0, ROWS), (-1, 0, ROWS), (1, 0, ROWS), (-2, 0, ROWS), (2, 0, ROWS)) + (
    (-3, 0, ROWS),
    (3, 0, ROWS),
    (-4, 0, ROWS // 2),
    (4, ROWS // 2, ROWS // 2),
)


def gather_rows(own, queries, weights):
    own = jnp.concatenate([own, pair_x(own)], axis=1)
    own, queries = barrier((own, queries))
    up1, down1 = along_z(own, 1), along_z(own, -1)
    up2, down2 = along_z(own, 2), along_z(own, -2)
    up2, down2, first_out = barrier((up2, down2, first_block(queries, weights)))
    up3, down3 = along_z(up2, 1), along_z(down2, -1)
    up4, down4 = along_z(up2[: ROWS // 2], 2), along_z(down2[ROWS // 2 :], -2)
    return [own, up1, down1, up2, down2, up3, down3, up4, down4], first_out


def pack_kernel(*refs):
    pieces = refs[:9]
    matrix, shared, sem = refs[9:]
    x, z, _ = place()
    copies = []
    for i, piece in enumerate(pieces):
        step, first, count = ORIGINS[i]
        rows = at_place(lax.rem(z + step + Z, Z) * ROWS + first, count)
        for j in range(4):
            side = lax.rem(x + j // 2, 2)
            target, size, offset = ((matrix, HALF, 0), (shared, QUARTER, HALF))[j % 2]
            copy = pltpu.make_async_copy(
                piece.at[:, pl.ds(j // 2 * WIDE + offset, size)],
                target.at[rows, at_place(side * size, size)],
                sem.at[i, j],
            )
            copy.start()
            copies.append(copy)
    for copy in copies:
        copy.wait()


def pack(pieces):
    return pl.pallas_call(
        pack_kernel,
        out_shape=(shape(DIM, FF), shape(DIM, HALF)),
        in_specs=[ANY] * 9,
        out_specs=(VMEM, VMEM),
        scratch_shapes=[pltpu.SemaphoreType.DMA((9, 4))],
        compiler_params=params(4),
        cost_estimate=cost(0, 3 << 20),
        name="pack",
    )(*pieces)


def gram_of(parts):
    gram = dot(parts[0], parts[0], ((1,), (1,)))
    for part in parts[1:]:
        gram += dot(part, part, ((1,), (1,)))
    gram = gram.astype(BF)
    gram_float = gram.astype(F32)
    level = jnp.sqrt(jnp.sum(gram_float * gram_float, keepdims=True)) + norm_eps
    half = 0.5 / level
    diagonal = lax.broadcasted_iota(jnp.int32, (DIM, DIM), 0) == lax.broadcasted_iota(
        jnp.int32, (DIM, DIM), 1
    )
    first_poly = (jnp.where(diagonal, 1.5, 0.0) - gram_float * half).astype(BF)
    return gram, first_poly, half, upd_scale / jnp.sqrt(level)


def combine(rows, offset, gram, first_poly, half):
    squared = dot(rows, first_poly, ((1,), (0,))).astype(BF)
    moved = dot(squared, gram, ((1,), (0,)))
    diagonal = lax.broadcasted_iota(jnp.int32, moved.shape, 0) + offset == lax.broadcasted_iota(
        jnp.int32, moved.shape, 1
    )
    second_poly = (jnp.where(diagonal, 1.5, 0.0) - moved * half).astype(BF)
    return dot(second_poly, first_poly, ((1,), (0,))).astype(BF)


def project_kernel(scaled, weights, query_own, query_core, query_far, query_far_core, out, w, q, sem):
    x, _, c = place()
    load = pltpu.make_async_copy(weights.at[c, x // 2], w, sem)
    load.start()
    tokens = query_own.shape[0]
    q[at_place(c * tokens, tokens), :] = query_own[...]
    q[at_place((1 - c) * tokens, tokens), :] = query_core[...]
    q[at_place((2 + c) * tokens, tokens), :] = query_far[...]
    q[at_place((3 - c) * tokens, tokens), :] = query_far_core[...]
    gram, first_poly, half, factor = gram_of([scaled[...]])
    combined = combine(first_poly, 0, gram, first_poly, half)
    update = dot(combined, scaled[...], ((1,), (0,))) * factor
    load.wait()
    renewed = (w[...].astype(F32) - update).astype(BF)
    out[...] = dot(q[...], renewed, ((1,), (0,)))


def project(scaled, weights, *queries):
    tokens = queries[0].shape[0]
    return pl.pallas_call(
        project_kernel,
        out_shape=shape(4 * tokens, FF, dtype=F32),
        in_specs=[VMEM, HBM] + [VMEM] * 4,
        out_specs=VMEM,
        scratch_shapes=[
            pltpu.VMEM((DIM, FF), BF),
            pltpu.VMEM((4 * tokens, DIM), BF),
            pltpu.SemaphoreType.DMA,
        ],
        compiler_params=params(16),
        cost_estimate=cost(22 * 10**8, 5 << 20),
        name="project",
    )(scaled, weights, *queries)


def third_kernel(mine, other, weights, out, scaled, w, poly, sem):
    x, _, c = place()
    rows = DIM // 2
    load = pltpu.make_async_copy(weights.at[2, x // 2, at_place(c * rows, rows)], w, sem)
    load.start()
    for side in range(2):
        cols = slice(side * QUARTER, (side + 1) * QUARTER)
        scaled[:, at_place(side * HALF + c * QUARTER, QUARTER)] = mine[:, cols]
        scaled[:, at_place(side * HALF + (1 - c) * QUARTER, QUARTER)] = other[:, cols]
    gram, first_poly, half, factor = gram_of([scaled[...]])
    poly[...] = first_poly
    combined = combine(poly[at_place(c * rows, rows), :], c * rows, gram, first_poly, half)
    update = dot(combined, scaled[...], ((1,), (0,))) * factor
    load.wait()
    out[...] = (w[...].astype(F32) - update).astype(BF)


def renew_third(mine, other, weights):
    rows = DIM // 2
    return pl.pallas_call(
        third_kernel,
        out_shape=shape(rows, FF),
        in_specs=[VMEM, VMEM, HBM],
        out_specs=VMEM,
        scratch_shapes=[
            pltpu.VMEM((DIM, FF), BF),
            pltpu.VMEM((rows, FF), BF),
            pltpu.VMEM((DIM, DIM), BF),
            pltpu.SemaphoreType.DMA,
        ],
        compiler_params=params(14),
        cost_estimate=cost(12 * 10**8, 4 << 20),
        name="renew_third",
    )(mine, other, weights)


def down_kernel(mine, other, rows, own, core, far, far_core, gated, result):
    _, _, c = place()

    @pl.when(c == 0)
    def _():
        first_proj = mine[...]
        gated[...] = (first_proj * jax.nn.sigmoid(first_proj) * other[...]).astype(BF)

    @pl.when(c == 1)
    def _():
        first_proj = other[...]
        gated[...] = (first_proj * jax.nn.sigmoid(first_proj) * mine[...]).astype(BF)

    result[...] = dot(gated[...], rows[...], ((1,), (1,))).astype(BF)
    tokens = own.shape[0]
    own[...] = result[at_place(c * tokens, tokens), :]
    core[...] = result[at_place((1 - c) * tokens, tokens), :]
    far[...] = result[at_place((2 + c) * tokens, tokens), :]
    far_core[...] = result[at_place((3 - c) * tokens, tokens), :]


def down(mine, other, rows):
    tokens = mine.shape[0] // 4
    part = shape(tokens, DIM // 2)
    return pl.pallas_call(
        down_kernel,
        out_shape=(part,) * 4,
        in_specs=[VMEM] * 3,
        out_specs=(VMEM,) * 4,
        scratch_shapes=[pltpu.VMEM((4 * tokens, FF), BF), pltpu.VMEM((4 * tokens, DIM // 2), BF)],
        compiler_params=params(8),
        cost_estimate=cost(3 * 10**8, 3 << 20),
        name="down",
    )(mine, other, rows)


def finish_kernel(first_out, own, core, far, far_core, out):
    x, _, c = place()
    half = DIM // 2
    here, there = x // 2 * DIM, (1 - x // 2) * DIM
    out[0] = first_out[...]
    out[1, :, at_place(here + c * half, half)] = own[...]
    out[1, :, at_place(here + (1 - c) * half, half)] = core[...]
    out[1, :, at_place(there + c * half, half)] = far[...]
    out[1, :, at_place(there + (1 - c) * half, half)] = far_core[...]


def finish(first_out, *parts):
    return pl.pallas_call(
        finish_kernel,
        out_shape=shape(2, *first_out.shape),
        in_specs=[VMEM] * 5,
        out_specs=VMEM,
        compiler_params=params(2),
        name="finish",
    )(first_out, *parts)


def body(queries, keys, values, rates, weights):
    own, far1, far2, far3, query_own, query_far = prepare(queries, keys, values, rates)
    own, weights = barrier((own, weights))
    got1, got2, got3 = along_x(far1, 1), along_x(far2, 2), along_x(far3, 3)
    got2, query_far, part = barrier((got2, query_far, load(weights)))
    query_far = mirror_x(query_far)
    got = [own, got1, got2, got3]
    got += [other_core(piece) for piece in got]
    parts, query_far = barrier((gradient(got, part), query_far))
    own, late_queries = reduce_rows(parts, query_own, query_far)
    pieces, first_out = gather_rows(own, queries, weights)
    matrix, shared = pack(pieces)
    shared_core = other_core(shared)
    projected = project(matrix, weights, *late_queries)
    projected, shared_core = barrier((projected, shared_core))
    projected_core = other_core(projected)
    rows = renew_third(shared, shared_core, weights)
    own, core, far, far_core = down(projected, projected_core, rows)
    return finish(first_out, own, other_core(core), mirror_x(far), mirror_x_core(far_core))


def solution(mesh):
    in_specs = (
        P(None, ("dp", "ctx"), None),
        P(None, ("dp", "ctx"), None),
        P(None, ("dp", "ctx"), None),
        P(None, None, ("dp", "ctx")),
        P(),
    )
    out_specs = P(None, ("dp", "ctx"), None)
    return jax.shard_map(body, mesh=mesh, in_specs=in_specs, out_specs=out_specs, check_vma=False)
```

```python
import jax
import jax.numpy as jnp
from jax import lax
from jax.experimental import pallas as pl
from jax.experimental.pallas import tpu as pltpu
from jax.sharding import PartitionSpec as P

X, Z, C = 4, 8, 2
DIM, FF = 512, 1024
HALF, QUARTER = FF // 2, FF // 4
WIDE = HALF + QUARTER
ROWS = DIM // Z
BF, F32 = jnp.bfloat16, jnp.float32
upd_scale = 2.0
norm_eps = 1e-07
VMEM = pl.BlockSpec(memory_space=pltpu.VMEM)
ANY = pl.BlockSpec(memory_space=pl.ANY)
HBM = pl.BlockSpec(memory_space=pltpu.HBM)


barrier = lax.optimization_barrier


def place():
    index = lax.axis_index("ctx")
    return index // (Z * C), (index // C) % Z, index % C


def move(array, to):
    perm = []
    for x in range(X):
        for z in range(Z):
            for c in range(C):
                tx, tz, tc = to(x, z, c)
                perm.append(((x * Z + z) * C + c, (tx % X * Z + tz % Z) * C + tc % C))
    return lax.ppermute(array, "ctx", perm)


def along_x(array, distance):
    return move(array, lambda x, z, c: (x + distance, z, c))


def along_z(array, distance):
    return move(array, lambda x, z, c: (x, z + distance, c))


def opposite_z(array):
    return move(array, lambda x, z, c: (x, z + 2 - 4 * c, c))


def pair_x(array):
    return move(array, lambda x, z, c: (x ^ 1, z, c))


def mirror_x(array):
    return move(array, lambda x, z, c: (X - 1 - x, z, c))


def mirror_x_core(array):
    return move(array, lambda x, z, c: (X - 1 - x, z, c + 1))


def other_core(array):
    return move(array, lambda x, z, c: (x, z, c + 1))


def dot(left, right, dims):
    return lax.dot_general(left, right, (dims, ((), ())), preferred_element_type=F32)


def shape(*dims, dtype=BF):
    return jax.ShapeDtypeStruct(dims, dtype)


def params(mib):
    return pltpu.CompilerParams(vmem_limit_bytes=mib << 20)


def cost(flops, size):
    return pl.CostEstimate(flops=flops, bytes_accessed=size, transcendentals=0)


def at_place(start, size):
    return pl.ds(pl.multiple_of(start, size), size)


def prepare_kernel(queries, keys, values, rates, *refs):
    own, far1, far2, far3, query_own, query_far, q, k, v, r, sem = refs
    copies = []
    for i, (source, target) in enumerate(
        ((rates, r), (values.at[0], v), (keys.at[0], k), (queries.at[1], q))
    ):
        copy = pltpu.make_async_copy(source, target, sem.at[i])
        copy.start()
        copies.append(copy)
    x, _, _ = place()
    tokens = k.shape[0]
    diagonal = lax.broadcasted_iota(jnp.int32, (tokens, tokens), 0) == lax.broadcasted_iota(
        jnp.int32, (tokens, tokens), 1
    )
    for copy in copies:
        copy.wait()
    for head in range(2):
        row = r[0, head : head + 1, :]
        rate = jnp.sum(jnp.where(diagonal, row, 0.0), axis=1, keepdims=True)
        cols = slice(head * DIM, (head + 1) * DIM)
        scaled = (v[:, cols].astype(F32) * rate).astype(BF)
        for distance, ref in enumerate((own, far1, far2, far3)):

            @pl.when(lax.rem(x + distance, X) // 2 == head)
            def _():
                ref[:tokens, :] = k[:, cols]
                ref[tokens:, :] = scaled

        @pl.when(x // 2 == head)
        def _():
            query_own[...] = q[:, cols]

        @pl.when(x // 2 != head)
        def _():
            query_far[...] = q[:, cols]


def prepare(queries, keys, values, rates):
    tokens = keys.shape[1]
    pair, half = shape(2 * tokens, DIM), shape(tokens, DIM)
    wide = pltpu.VMEM((tokens, 2 * DIM), BF)
    return pl.pallas_call(
        prepare_kernel,
        out_shape=(pair, pair, pair, pair, half, half),
        in_specs=[HBM] * 4,
        out_specs=(VMEM,) * 6,
        scratch_shapes=[
            wide,
            wide,
            wide,
            pltpu.VMEM(rates.shape, F32),
            pltpu.SemaphoreType.DMA((4,)),
        ],
        name="prepare",
    )(queries, keys, values, rates)


def first_kernel(queries, weights, out, q, w, sem, query_sem):
    load_query = pltpu.make_async_copy(queries.at[0], q, query_sem)
    load_query.start()
    copies = []
    for head in range(2):
        for m in range(3):
            copy = pltpu.make_async_copy(weights.at[m, head], w.at[head, m], sem.at[head, m])
            copy.start()
            copies.append(copy)
    load_query.wait()
    for head in range(2):
        cols = slice(head * DIM, (head + 1) * DIM)
        query = q[:, cols]
        copies[3 * head].wait()
        first_proj = dot(query, w[head, 0], ((1,), (0,)))
        copies[3 * head + 1].wait()
        third_proj = dot(query, w[head, 1], ((1,), (0,)))
        gated = (first_proj * jax.nn.sigmoid(first_proj) * third_proj).astype(BF)
        copies[3 * head + 2].wait()
        out[:, cols] = dot(gated, w[head, 2], ((1,), (1,))).astype(BF)


def first_block(queries, weights):
    tokens = queries.shape[1]
    return pl.pallas_call(
        first_kernel,
        out_shape=shape(tokens, 2 * DIM),
        in_specs=[HBM, HBM],
        out_specs=VMEM,
        scratch_shapes=[
            pltpu.VMEM((tokens, 2 * DIM), BF),
            pltpu.VMEM((2, 3, DIM, FF), BF),
            pltpu.SemaphoreType.DMA((2, 3)),
            pltpu.SemaphoreType.DMA,
        ],
        compiler_params=params(12),
        cost_estimate=cost(12 * tokens * DIM * FF, 7 << 20),
        name="first_block",
    )(queries, weights)


def load_kernel(weights, out, sem):
    x, _, _ = place()
    copies = []
    for m in range(3):
        copy = pltpu.make_async_copy(
            weights.at[m, x // 2, :, at_place(lax.rem(x, 2) * HALF, HALF)], out.at[m], sem.at[m]
        )
        copy.start()
        copies.append(copy)
    for copy in copies:
        copy.wait()


def load(weights):
    return pl.pallas_call(
        load_kernel,
        out_shape=shape(3, DIM, HALF),
        in_specs=[HBM],
        out_specs=VMEM,
        scratch_shapes=[pltpu.SemaphoreType.DMA((3,))],
        compiler_params=params(2),
        cost_estimate=cost(0, 3 << 20),
        name="load",
    )(weights)


def gradient_kernel(*refs):
    pieces, w = refs[:8], refs[8]
    own, up, down, keep_up, keep_down, far = refs[9:15]
    k, v, d, gated, total = refs[15:]
    _, z, c = place()
    tokens = pieces[0].shape[0] // 2
    for i, piece in enumerate(pieces):
        k[i * tokens : (i + 1) * tokens, :] = piece[:tokens, :]
        v[i * tokens : (i + 1) * tokens, :] = piece[tokens:, :]
    key_first = dot(k[...], w[0], ((1,), (0,)))
    key_third = dot(k[...], w[1], ((1,), (0,)))
    back_grad = -dot(v[...], w[2], ((1,), (0,)))
    sig = jax.nn.sigmoid(key_first)
    key_act = key_first * sig

    @pl.when(c == 0)
    def _():
        d[...] = (back_grad * key_third * sig * (1.0 + key_first * (1.0 - sig))).astype(BF)
        gated[...] = (key_act[:, :QUARTER] * key_third[:, :QUARTER]).astype(BF)

    @pl.when(c == 1)
    def _():
        d[...] = (back_grad * key_act).astype(BF)
        gated[...] = (key_act[:, QUARTER:] * key_third[:, QUARTER:]).astype(BF)

    total[:, :HALF] = dot(k[...], d[...], ((0,), (0,)))
    total[:, HALF:] = -dot(v[...], gated[...], ((0,), (0,)))

    def rows(distance):
        return total[at_place(lax.rem(z + distance + Z, Z) * ROWS, ROWS), :]

    own[...] = rows(0)
    up[:ROWS, :] = rows(1).astype(BF)
    up[ROWS:, :] = rows(3).astype(BF)
    down[:ROWS, :] = rows(-1).astype(BF)
    down[ROWS:, :] = rows(-3).astype(BF)
    keep_up[...] = rows(2)
    keep_down[...] = rows(-2)
    far[...] = rows(4).astype(BF)


def gradient(pieces, weights):
    tokens = 8 * pieces[0].shape[0] // 2
    kept, sent, far = shape(ROWS, WIDE, dtype=F32), shape(2 * ROWS, WIDE), shape(ROWS, WIDE)
    return pl.pallas_call(
        gradient_kernel,
        out_shape=(kept, sent, sent, kept, kept, far),
        in_specs=[VMEM] * 9,
        out_specs=(VMEM,) * 6,
        scratch_shapes=[
            pltpu.VMEM((tokens, DIM), BF),
            pltpu.VMEM((tokens, DIM), BF),
            pltpu.VMEM((tokens, HALF), BF),
            pltpu.VMEM((tokens, QUARTER), BF),
            pltpu.VMEM((DIM, WIDE), F32),
        ],
        compiler_params=params(16),
        cost_estimate=cost(10 * tokens * DIM * HALF, 6 << 20),
        name="gradient",
    )(*pieces, weights)


def middle_kernel(keep_up, keep_down, got_up, got_down, far, up, down):
    _, _, c = place()
    total_up = keep_up[...] + got_up[ROWS:, :].astype(F32)
    total_down = keep_down[...] + got_down[ROWS:, :].astype(F32)
    last = far[...].astype(F32)

    @pl.when(c == 0)
    def _():
        up[...] = (total_up + last).astype(BF)
        down[...] = total_down.astype(BF)

    @pl.when(c == 1)
    def _():
        up[...] = total_up.astype(BF)
        down[...] = (total_down + last).astype(BF)


def middle(*args):
    return pl.pallas_call(
        middle_kernel,
        out_shape=(shape(ROWS, WIDE), shape(ROWS, WIDE)),
        in_specs=[VMEM] * 5,
        out_specs=(VMEM, VMEM),
        compiler_params=params(3),
        name="middle",
    )(*args)


def total_kernel(own, a, b, c, d, out):
    total = own[...] + a[:ROWS, :].astype(F32) + b[:ROWS, :].astype(F32) + c[...].astype(F32)
    out[...] = (total + d[...].astype(F32)).astype(BF)


def add_up(*args):
    return pl.pallas_call(
        total_kernel,
        out_shape=shape(ROWS, WIDE),
        in_specs=[VMEM] * 5,
        out_specs=VMEM,
        compiler_params=params(3),
        name="add_up",
    )(*args)


def reduce_rows(parts):
    own, up, down, keep_up, keep_down, far = parts
    far = opposite_z(far)
    got_up, got_down = along_z(up, 1), along_z(down, -1)
    up, down = middle(keep_up, keep_down, got_up, got_down, far)
    return add_up(own, got_up, got_down, along_z(up, 2), along_z(down, -2))


ORIGINS = (0, -1, 1, -2, 2, -3, 3, 4)


def gather_rows(own, queries, weights):
    _, _, c = place()
    own, queries = barrier((own, queries))
    up1, down1 = along_z(own, 1), along_z(own, -1)
    up2, down2 = along_z(own, 2), along_z(own, -2)
    up2, down2, first_out = barrier((up2, down2, first_block(queries, weights)))
    up3, down3 = along_z(up2, 1), along_z(down2, -1)
    far = opposite_z(jnp.where(c == 0, up2, down2))
    return [own, up1, down1, up2, down2, up3, down3, far], first_out


def pack_kernel(*refs):
    pieces = refs[:8]
    matrix, shared, sem = refs[8:]
    x, z, _ = place()
    copies = []
    for i, piece in enumerate(pieces):
        rows = at_place(lax.rem(z + ORIGINS[i] + Z, Z) * ROWS, ROWS)
        for j in range(4):
            side = lax.rem(x + j // 2, 2)
            target, size, offset = ((matrix, HALF, 0), (shared, QUARTER, HALF))[j % 2]
            copy = pltpu.make_async_copy(
                piece.at[:, pl.ds(j // 2 * WIDE + offset, size)],
                target.at[rows, at_place(side * size, size)],
                sem.at[i, j],
            )
            copy.start()
            copies.append(copy)
    for copy in copies:
        copy.wait()


def pack(pieces):
    return pl.pallas_call(
        pack_kernel,
        out_shape=(shape(DIM, FF), shape(DIM, HALF)),
        in_specs=[ANY] * 8,
        out_specs=(VMEM, VMEM),
        scratch_shapes=[pltpu.SemaphoreType.DMA((8, 4))],
        compiler_params=params(4),
        cost_estimate=cost(0, 3 << 20),
        name="pack",
    )(*pieces)


def gram_of(parts):
    gram = dot(parts[0], parts[0], ((1,), (1,)))
    for part in parts[1:]:
        gram += dot(part, part, ((1,), (1,)))
    gram = gram.astype(BF)
    gram_float = gram.astype(F32)
    level = jnp.sqrt(jnp.sum(gram_float * gram_float, keepdims=True)) + norm_eps
    half = 0.5 / level
    diagonal = lax.broadcasted_iota(jnp.int32, (DIM, DIM), 0) == lax.broadcasted_iota(
        jnp.int32, (DIM, DIM), 1
    )
    first_poly = (jnp.where(diagonal, 1.5, 0.0) - gram_float * half).astype(BF)
    return gram, first_poly, half, upd_scale / jnp.sqrt(level)


def combine(rows, offset, gram, first_poly, half):
    squared = dot(rows, first_poly, ((1,), (0,))).astype(BF)
    moved = dot(squared, gram, ((1,), (0,)))
    diagonal = lax.broadcasted_iota(jnp.int32, moved.shape, 0) + offset == lax.broadcasted_iota(
        jnp.int32, moved.shape, 1
    )
    second_poly = (jnp.where(diagonal, 1.5, 0.0) - moved * half).astype(BF)
    return dot(second_poly, first_poly, ((1,), (0,))).astype(BF)


def project_kernel(scaled, weights, query_own, query_core, query_far, query_far_core, out, w, q, sem):
    x, _, c = place()
    load = pltpu.make_async_copy(weights.at[c, x // 2], w, sem)
    load.start()
    tokens = query_own.shape[0]
    q[at_place(c * tokens, tokens), :] = query_own[...]
    q[at_place((1 - c) * tokens, tokens), :] = query_core[...]
    q[at_place((2 + c) * tokens, tokens), :] = query_far[...]
    q[at_place((3 - c) * tokens, tokens), :] = query_far_core[...]
    gram, first_poly, half, factor = gram_of([scaled[...]])
    combined = combine(first_poly, 0, gram, first_poly, half)
    update = dot(combined, scaled[...], ((1,), (0,))) * factor
    load.wait()
    renewed = (w[...].astype(F32) - update).astype(BF)
    out[...] = dot(q[...], renewed, ((1,), (0,)))


def project(scaled, weights, *queries):
    tokens = queries[0].shape[0]
    return pl.pallas_call(
        project_kernel,
        out_shape=shape(4 * tokens, FF, dtype=F32),
        in_specs=[VMEM, HBM] + [VMEM] * 4,
        out_specs=VMEM,
        scratch_shapes=[
            pltpu.VMEM((DIM, FF), BF),
            pltpu.VMEM((4 * tokens, DIM), BF),
            pltpu.SemaphoreType.DMA,
        ],
        compiler_params=params(16),
        cost_estimate=cost(22 * 10**8, 5 << 20),
        name="project",
    )(scaled, weights, *queries)


def third_kernel(mine, other, weights, out, scaled, w, poly, sem):
    x, _, c = place()
    rows = DIM // 2
    load = pltpu.make_async_copy(weights.at[2, x // 2, at_place(c * rows, rows)], w, sem)
    load.start()
    for side in range(2):
        cols = slice(side * QUARTER, (side + 1) * QUARTER)
        scaled[:, at_place(side * HALF + c * QUARTER, QUARTER)] = mine[:, cols]
        scaled[:, at_place(side * HALF + (1 - c) * QUARTER, QUARTER)] = other[:, cols]
    gram, first_poly, half, factor = gram_of([scaled[...]])
    poly[...] = first_poly
    combined = combine(poly[at_place(c * rows, rows), :], c * rows, gram, first_poly, half)
    update = dot(combined, scaled[...], ((1,), (0,))) * factor
    load.wait()
    out[...] = (w[...].astype(F32) - update).astype(BF)


def renew_third(mine, other, weights):
    rows = DIM // 2
    return pl.pallas_call(
        third_kernel,
        out_shape=shape(rows, FF),
        in_specs=[VMEM, VMEM, HBM],
        out_specs=VMEM,
        scratch_shapes=[
            pltpu.VMEM((DIM, FF), BF),
            pltpu.VMEM((rows, FF), BF),
            pltpu.VMEM((DIM, DIM), BF),
            pltpu.SemaphoreType.DMA,
        ],
        compiler_params=params(14),
        cost_estimate=cost(12 * 10**8, 4 << 20),
        name="renew_third",
    )(mine, other, weights)


def down_kernel(mine, other, rows, own, core, far, far_core, gated, result):
    _, _, c = place()

    @pl.when(c == 0)
    def _():
        first_proj = mine[...]
        gated[...] = (first_proj * jax.nn.sigmoid(first_proj) * other[...]).astype(BF)

    @pl.when(c == 1)
    def _():
        first_proj = other[...]
        gated[...] = (first_proj * jax.nn.sigmoid(first_proj) * mine[...]).astype(BF)

    result[...] = dot(gated[...], rows[...], ((1,), (1,))).astype(BF)
    tokens = own.shape[0]
    own[...] = result[at_place(c * tokens, tokens), :]
    core[...] = result[at_place((1 - c) * tokens, tokens), :]
    far[...] = result[at_place((2 + c) * tokens, tokens), :]
    far_core[...] = result[at_place((3 - c) * tokens, tokens), :]


def down(mine, other, rows):
    tokens = mine.shape[0] // 4
    part = shape(tokens, DIM // 2)
    return pl.pallas_call(
        down_kernel,
        out_shape=(part,) * 4,
        in_specs=[VMEM] * 3,
        out_specs=(VMEM,) * 4,
        scratch_shapes=[pltpu.VMEM((4 * tokens, FF), BF), pltpu.VMEM((4 * tokens, DIM // 2), BF)],
        compiler_params=params(8),
        cost_estimate=cost(3 * 10**8, 3 << 20),
        name="down",
    )(mine, other, rows)


def finish_kernel(first_out, own, core, far, far_core, out):
    x, _, c = place()
    half = DIM // 2
    here, there = x // 2 * DIM, (1 - x // 2) * DIM
    out[0] = first_out[...]
    out[1, :, at_place(here + c * half, half)] = own[...]
    out[1, :, at_place(here + (1 - c) * half, half)] = core[...]
    out[1, :, at_place(there + c * half, half)] = far[...]
    out[1, :, at_place(there + (1 - c) * half, half)] = far_core[...]


def finish(first_out, *parts):
    return pl.pallas_call(
        finish_kernel,
        out_shape=shape(2, *first_out.shape),
        in_specs=[VMEM] * 5,
        out_specs=VMEM,
        compiler_params=params(2),
        name="finish",
    )(first_out, *parts)


def body(queries, keys, values, rates, weights):
    own, far1, far2, far3, query_own, query_far = prepare(queries, keys, values, rates)
    own, weights = barrier((own, weights))
    got1, got2, got3 = along_x(far1, 1), along_x(far2, 2), along_x(far3, 3)
    got2, query_own, part = barrier((got2, query_own, load(weights)))
    got = [own, got1, got2, got3]
    got += [other_core(piece) for piece in got]
    got, query_core = barrier((got, other_core(query_own)))
    own, query_far = barrier((reduce_rows(gradient(got, part)), query_far))
    own, near, query_far, query_far_core = barrier(
        (own, pair_x(own), mirror_x(query_far), mirror_x_core(query_far))
    )
    pieces, first_out = gather_rows(jnp.concatenate([own, near], axis=1), queries, weights)
    matrix, shared = pack(pieces)
    shared_core = other_core(shared)
    projected = project(matrix, weights, query_own, query_core, query_far, query_far_core)
    projected, shared_core = barrier((projected, shared_core))
    projected_core = other_core(projected)
    rows = renew_third(shared, shared_core, weights)
    own, core, far, far_core = down(projected, projected_core, rows)
    return finish(first_out, own, other_core(core), mirror_x(far), mirror_x_core(far_core))


def solution(mesh):
    in_specs = (
        P(None, ("dp", "ctx"), None),
        P(None, ("dp", "ctx"), None),
        P(None, ("dp", "ctx"), None),
        P(None, None, ("dp", "ctx")),
        P(),
    )
    out_specs = P(None, ("dp", "ctx"), None)
    return jax.shard_map(body, mesh=mesh, in_specs=in_specs, out_specs=out_specs, check_vma=False)
```

```python
import jax
import jax.numpy as jnp
from jax import lax
from jax.experimental import pallas as pl
from jax.experimental.pallas import tpu as pltpu
from jax.sharding import PartitionSpec as P

X, Z, C = 4, 8, 2
DIM, FF = 512, 1024
HALF, QUARTER = FF // 2, FF // 4
WIDE = HALF + QUARTER
ROWS = DIM // Z
BF, F32 = jnp.bfloat16, jnp.float32
upd_scale = 2.0
norm_eps = 1e-07
VMEM = pl.BlockSpec(memory_space=pltpu.VMEM)
ANY = pl.BlockSpec(memory_space=pl.ANY)
HBM = pl.BlockSpec(memory_space=pltpu.HBM)


barrier = lax.optimization_barrier


def place():
    index = lax.axis_index("ctx")
    return index // (Z * C), (index // C) % Z, index % C


def move(array, to):
    perm = []
    for x in range(X):
        for z in range(Z):
            for c in range(C):
                tx, tz, tc = to(x, z, c)
                perm.append(((x * Z + z) * C + c, (tx % X * Z + tz % Z) * C + tc % C))
    return lax.ppermute(array, "ctx", perm)


def along_x(array, distance):
    return move(array, lambda x, z, c: (x + distance, z, c))


def along_z(array, distance):
    return move(array, lambda x, z, c: (x, z + distance, c))


def pair_x(array):
    return move(array, lambda x, z, c: (x ^ 1, z, c))


def mirror_x(array):
    return move(array, lambda x, z, c: (X - 1 - x, z, c))


def other_core(array):
    return move(array, lambda x, z, c: (x, z, c + 1))


def dot(left, right, dims):
    return lax.dot_general(left, right, (dims, ((), ())), preferred_element_type=F32)


def shape(*dims, dtype=BF):
    return jax.ShapeDtypeStruct(dims, dtype)


def params(mib):
    return pltpu.CompilerParams(vmem_limit_bytes=mib << 20)


def cost(flops, size):
    return pl.CostEstimate(flops=flops, bytes_accessed=size, transcendentals=0)


def at_place(start, size):
    return pl.ds(pl.multiple_of(start, size), size)


def prepare_kernel(queries, keys, values, rates, *refs):
    own, far1, far2, far3, query_own, query_far, q, k, v, r, sem = refs
    copies = []
    for i, (source, target) in enumerate(
        ((rates, r), (values.at[0], v), (keys.at[0], k), (queries.at[1], q))
    ):
        copy = pltpu.make_async_copy(source, target, sem.at[i])
        copy.start()
        copies.append(copy)
    x, _, _ = place()
    tokens = k.shape[0]
    diagonal = lax.broadcasted_iota(jnp.int32, (tokens, tokens), 0) == lax.broadcasted_iota(
        jnp.int32, (tokens, tokens), 1
    )
    for copy in copies:
        copy.wait()
    for head in range(2):
        row = r[0, head : head + 1, :]
        rate = jnp.sum(jnp.where(diagonal, row, 0.0), axis=1, keepdims=True)
        cols = slice(head * DIM, (head + 1) * DIM)
        scaled = (v[:, cols].astype(F32) * rate).astype(BF)
        for distance, ref in enumerate((own, far1, far2, far3)):

            @pl.when(lax.rem(x + distance, X) // 2 == head)
            def _():
                ref[:tokens, :] = k[:, cols]
                ref[tokens:, :] = scaled

        @pl.when(x // 2 == head)
        def _():
            query_own[...] = q[:, cols]

        @pl.when(x // 2 != head)
        def _():
            query_far[...] = q[:, cols]


def prepare(queries, keys, values, rates):
    tokens = keys.shape[1]
    pair, half = shape(2 * tokens, DIM), shape(tokens, DIM)
    wide = pltpu.VMEM((tokens, 2 * DIM), BF)
    return pl.pallas_call(
        prepare_kernel,
        out_shape=(pair, pair, pair, pair, half, half),
        in_specs=[HBM] * 4,
        out_specs=(VMEM,) * 6,
        scratch_shapes=[
            wide,
            wide,
            wide,
            pltpu.VMEM(rates.shape, F32),
            pltpu.SemaphoreType.DMA((4,)),
        ],
        name="prepare",
    )(queries, keys, values, rates)


def first_kernel(queries, weights, out, q, w, sem, query_sem):
    load_query = pltpu.make_async_copy(queries.at[0], q, query_sem)
    load_query.start()
    copies = []
    for head in range(2):
        for m in range(3):
            copy = pltpu.make_async_copy(weights.at[m, head], w.at[head, m], sem.at[head, m])
            copy.start()
            copies.append(copy)
    load_query.wait()
    for head in range(2):
        cols = slice(head * DIM, (head + 1) * DIM)
        query = q[:, cols]
        copies[3 * head].wait()
        first_proj = dot(query, w[head, 0], ((1,), (0,)))
        copies[3 * head + 1].wait()
        third_proj = dot(query, w[head, 1], ((1,), (0,)))
        gated = (first_proj * jax.nn.sigmoid(first_proj) * third_proj).astype(BF)
        copies[3 * head + 2].wait()
        out[:, cols] = dot(gated, w[head, 2], ((1,), (1,))).astype(BF)


def first_block(queries, weights):
    tokens = queries.shape[1]
    return pl.pallas_call(
        first_kernel,
        out_shape=shape(tokens, 2 * DIM),
        in_specs=[HBM, HBM],
        out_specs=VMEM,
        scratch_shapes=[
            pltpu.VMEM((tokens, 2 * DIM), BF),
            pltpu.VMEM((2, 3, DIM, FF), BF),
            pltpu.SemaphoreType.DMA((2, 3)),
            pltpu.SemaphoreType.DMA,
        ],
        compiler_params=params(12),
        cost_estimate=cost(12 * tokens * DIM * FF, 7 << 20),
        name="first_block",
    )(queries, weights)


def load_kernel(weights, out, sem):
    x, _, _ = place()
    copies = []
    for m in range(3):
        copy = pltpu.make_async_copy(
            weights.at[m, x // 2, :, at_place(lax.rem(x, 2) * HALF, HALF)], out.at[m], sem.at[m]
        )
        copy.start()
        copies.append(copy)
    for copy in copies:
        copy.wait()


def load(weights):
    return pl.pallas_call(
        load_kernel,
        out_shape=shape(3, DIM, HALF),
        in_specs=[HBM],
        out_specs=VMEM,
        scratch_shapes=[pltpu.SemaphoreType.DMA((3,))],
        compiler_params=params(2),
        cost_estimate=cost(0, 3 << 20),
        name="load",
    )(weights)


def gradient_kernel(*refs):
    pieces, w = refs[:8], refs[8]
    own, up, down, keep_up, keep_down, far_up, far_down = refs[9:16]
    k, v, d, gated, total = refs[16:]
    _, z, c = place()
    tokens = pieces[0].shape[0] // 2
    for i, piece in enumerate(pieces):
        k[i * tokens : (i + 1) * tokens, :] = piece[:tokens, :]
        v[i * tokens : (i + 1) * tokens, :] = piece[tokens:, :]
    key_first = dot(k[...], w[0], ((1,), (0,)))
    key_third = dot(k[...], w[1], ((1,), (0,)))
    back_grad = -dot(v[...], w[2], ((1,), (0,)))
    sig = jax.nn.sigmoid(key_first)
    key_act = key_first * sig

    @pl.when(c == 0)
    def _():
        d[...] = (back_grad * key_third * sig * (1.0 + key_first * (1.0 - sig))).astype(BF)
        gated[...] = (key_act[:, :QUARTER] * key_third[:, :QUARTER]).astype(BF)

    @pl.when(c == 1)
    def _():
        d[...] = (back_grad * key_act).astype(BF)
        gated[...] = (key_act[:, QUARTER:] * key_third[:, QUARTER:]).astype(BF)

    total[:, :HALF] = dot(k[...], d[...], ((0,), (0,)))
    total[:, HALF:] = -dot(v[...], gated[...], ((0,), (0,)))

    def rows(distance):
        return total[at_place(lax.rem(z + distance + Z, Z) * ROWS, ROWS), :]

    own[...] = rows(0)
    up[:ROWS, :] = rows(1).astype(BF)
    up[ROWS:, :] = rows(3).astype(BF)
    down[:ROWS, :] = rows(-1).astype(BF)
    down[ROWS:, :] = rows(-3).astype(BF)
    keep_up[...] = rows(2)
    keep_down[...] = rows(-2)
    far = rows(4).astype(BF)
    far_up[...] = far[: ROWS // 2]
    far_down[...] = far[ROWS // 2 :]


def gradient(pieces, weights):
    tokens = 8 * pieces[0].shape[0] // 2
    kept, sent, half = shape(ROWS, WIDE, dtype=F32), shape(2 * ROWS, WIDE), shape(ROWS // 2, WIDE)
    return pl.pallas_call(
        gradient_kernel,
        out_shape=(kept, sent, sent, kept, kept, half, half),
        in_specs=[VMEM] * 9,
        out_specs=(VMEM,) * 7,
        scratch_shapes=[
            pltpu.VMEM((tokens, DIM), BF),
            pltpu.VMEM((tokens, DIM), BF),
            pltpu.VMEM((tokens, HALF), BF),
            pltpu.VMEM((tokens, QUARTER), BF),
            pltpu.VMEM((DIM, WIDE), F32),
        ],
        compiler_params=params(16),
        cost_estimate=cost(10 * tokens * DIM * HALF, 6 << 20),
        name="gradient",
    )(*pieces, weights)


def middle_kernel(keep_up, keep_down, got_up, got_down, far_up, far_down, up, down):
    half = ROWS // 2
    total = keep_up[...] + got_up[ROWS:, :].astype(F32)
    up[:half, :] = (total[:half] + far_up[...].astype(F32)).astype(BF)
    up[half:, :] = total[half:].astype(BF)
    total = keep_down[...] + got_down[ROWS:, :].astype(F32)
    down[:half, :] = total[:half].astype(BF)
    down[half:, :] = (total[half:] + far_down[...].astype(F32)).astype(BF)


def middle(*args):
    return pl.pallas_call(
        middle_kernel,
        out_shape=(shape(ROWS, WIDE), shape(ROWS, WIDE)),
        in_specs=[VMEM] * 6,
        out_specs=(VMEM, VMEM),
        compiler_params=params(3),
        name="middle",
    )(*args)


def total_kernel(own, a, b, c, d, out):
    total = own[...] + a[:ROWS, :].astype(F32) + b[:ROWS, :].astype(F32) + c[...].astype(F32)
    out[...] = (total + d[...].astype(F32)).astype(BF)


def add_up(*args):
    return pl.pallas_call(
        total_kernel,
        out_shape=shape(ROWS, WIDE),
        in_specs=[VMEM] * 5,
        out_specs=VMEM,
        compiler_params=params(3),
        name="add_up",
    )(*args)


def reduce_rows(parts, query_own, query_far):
    own, up, down, keep_up, keep_down, far_up, far_down = parts
    far_up, far_down = along_z(far_up, 2), along_z(far_down, -2)
    got_up, got_down = along_z(up, 1), along_z(down, -1)
    up, down = middle(keep_up, keep_down, got_up, got_down, far_up, far_down)
    up, down, query_own, query_far = barrier((up, down, query_own, query_far))
    up, down = along_z(up, 2), along_z(down, -2)
    up, down, query_core, query_far_core = barrier(
        (up, down, other_core(query_own), other_core(query_far))
    )
    return add_up(own, got_up, got_down, up, down), (query_own, query_core, query_far, query_far_core)


ORIGINS = ((0, 0, ROWS), (-1, 0, ROWS), (1, 0, ROWS), (-2, 0, ROWS), (2, 0, ROWS)) + (
    (-3, 0, ROWS),
    (3, 0, ROWS),
    (-4, 0, ROWS // 2),
    (4, ROWS // 2, ROWS // 2),
)


def gather_rows(own, queries, weights):
    own = jnp.concatenate([own, pair_x(own)], axis=1)
    own, queries = barrier((own, queries))
    up1, down1 = along_z(own, 1), along_z(own, -1)
    up2, down2 = along_z(own, 2), along_z(own, -2)
    up2, down2, first_out = barrier((up2, down2, first_block(queries, weights)))
    up3, down3 = along_z(up2, 1), along_z(down2, -1)
    up4, down4 = along_z(up2[: ROWS // 2], 2), along_z(down2[ROWS // 2 :], -2)
    return [own, up1, down1, up2, down2, up3, down3, up4, down4], first_out


def pack_kernel(*refs):
    pieces = refs[:9]
    matrix, shared, sem = refs[9:]
    x, z, _ = place()
    copies = []
    for i, piece in enumerate(pieces):
        step, first, count = ORIGINS[i]
        rows = at_place(lax.rem(z + step + Z, Z) * ROWS + first, count)
        for j in range(4):
            side = lax.rem(x + j // 2, 2)
            target, size, offset = ((matrix, HALF, 0), (shared, QUARTER, HALF))[j % 2]
            copy = pltpu.make_async_copy(
                piece.at[:, pl.ds(j // 2 * WIDE + offset, size)],
                target.at[rows, at_place(side * size, size)],
                sem.at[i, j],
            )
            copy.start()
            copies.append(copy)
    for copy in copies:
        copy.wait()


def pack(pieces):
    return pl.pallas_call(
        pack_kernel,
        out_shape=(shape(DIM, FF), shape(DIM, HALF)),
        in_specs=[ANY] * 9,
        out_specs=(VMEM, VMEM),
        scratch_shapes=[pltpu.SemaphoreType.DMA((9, 4))],
        compiler_params=params(4),
        cost_estimate=cost(0, 3 << 20),
        name="pack",
    )(*pieces)


def diagonal(value):
    return jnp.where(
        lax.broadcasted_iota(jnp.int32, (DIM, DIM), 0)
        == lax.broadcasted_iota(jnp.int32, (DIM, DIM), 1),
        value,
        0.0,
    )


def gram_of(scaled):
    gram = dot(scaled, scaled, ((1,), (1,))).astype(BF)
    gram_float = gram.astype(F32)
    level = jnp.sqrt(jnp.sum(gram_float * gram_float, keepdims=True)) + norm_eps
    half = 0.5 / level
    first_poly = (diagonal(1.5) - gram_float * half).astype(BF)
    return gram, first_poly, half, upd_scale / jnp.sqrt(level)


def combine(gram, first_poly, half):
    squared = dot(first_poly, first_poly, ((1,), (0,))).astype(BF)
    moved = dot(squared, gram, ((1,), (0,)))
    second_poly = (diagonal(1.5) - moved * half).astype(BF)
    return dot(second_poly, first_poly, ((1,), (0,))).astype(BF)


def project_kernel(scaled, weights, query_own, query_far, query_core, query_far_core, *refs):
    mine, theirs, w, q, sem = refs
    x, _, c = place()
    load = pltpu.make_async_copy(weights.at[c, x // 2], w, sem)
    load.start()
    tokens = query_own.shape[0]
    for i, query in enumerate((query_own, query_far, query_core, query_far_core)):
        q[i * tokens : (i + 1) * tokens, :] = query[...]
    gram, first_poly, half, factor = gram_of(scaled[...])
    combined = combine(gram, first_poly, half)
    update = dot(combined, scaled[...], ((1,), (0,))) * factor
    load.wait()
    renewed = (w[...].astype(F32) - update).astype(BF)
    projected = dot(q[...], renewed, ((1,), (0,)))
    mine[...] = projected[: 2 * tokens]
    theirs[...] = projected[2 * tokens :]


def project(scaled, weights, *queries):
    tokens = queries[0].shape[0]
    half = shape(2 * tokens, FF, dtype=F32)
    return pl.pallas_call(
        project_kernel,
        out_shape=(half, half),
        in_specs=[VMEM, HBM] + [VMEM] * 4,
        out_specs=(VMEM, VMEM),
        scratch_shapes=[
            pltpu.VMEM((DIM, FF), BF),
            pltpu.VMEM((4 * tokens, DIM), BF),
            pltpu.SemaphoreType.DMA,
        ],
        compiler_params=params(16),
        cost_estimate=cost(22 * 10**8, 5 << 20),
        name="project",
    )(scaled, weights, *queries)


def third_kernel(mine, other, weights, out, scaled, w, sem):
    x, _, c = place()
    load = pltpu.make_async_copy(weights.at[2, x // 2], w, sem)
    load.start()
    for side in range(2):
        cols = slice(side * QUARTER, (side + 1) * QUARTER)
        scaled[:, at_place(side * HALF + c * QUARTER, QUARTER)] = mine[:, cols]
        scaled[:, at_place(side * HALF + (1 - c) * QUARTER, QUARTER)] = other[:, cols]
    gram, first_poly, half, factor = gram_of(scaled[...])
    combined = combine(gram, first_poly, half)
    update = dot(combined, scaled[...], ((1,), (0,))) * factor
    load.wait()
    out[...] = (w[...].astype(F32) - update).astype(BF)


def renew_third(mine, other, weights):
    return pl.pallas_call(
        third_kernel,
        out_shape=shape(DIM, FF),
        in_specs=[VMEM, VMEM, HBM],
        out_specs=VMEM,
        scratch_shapes=[
            pltpu.VMEM((DIM, FF), BF),
            pltpu.VMEM((DIM, FF), BF),
            pltpu.SemaphoreType.DMA,
        ],
        compiler_params=params(16),
        cost_estimate=cost(19 * 10**8, 4 << 20),
        name="renew_third",
    )(mine, other, weights)


def down_kernel(mine, other, weights, own, far, gated):
    _, _, c = place()

    @pl.when(c == 0)
    def _():
        first_proj = mine[...]
        gated[...] = (first_proj * jax.nn.sigmoid(first_proj) * other[...]).astype(BF)

    @pl.when(c == 1)
    def _():
        first_proj = other[...]
        gated[...] = (first_proj * jax.nn.sigmoid(first_proj) * mine[...]).astype(BF)

    result = dot(gated[...], weights[...], ((1,), (1,))).astype(BF)
    tokens = own.shape[0]
    own[...] = result[:tokens]
    far[...] = result[tokens:]


def down(mine, other, weights):
    tokens = mine.shape[0] // 2
    part = shape(tokens, DIM)
    return pl.pallas_call(
        down_kernel,
        out_shape=(part, part),
        in_specs=[VMEM] * 3,
        out_specs=(VMEM, VMEM),
        scratch_shapes=[pltpu.VMEM((2 * tokens, FF), BF)],
        compiler_params=params(8),
        cost_estimate=cost(3 * 10**8, 3 << 20),
        name="down",
    )(mine, other, weights)


def finish_kernel(first_out, own, far, out):
    x, _, _ = place()
    out[0] = first_out[...]
    out[1, :, at_place(x // 2 * DIM, DIM)] = own[...]
    out[1, :, at_place((1 - x // 2) * DIM, DIM)] = far[...]


def finish(first_out, own, far):
    return pl.pallas_call(
        finish_kernel,
        out_shape=shape(2, *first_out.shape),
        in_specs=[VMEM] * 3,
        out_specs=VMEM,
        compiler_params=params(2),
        name="finish",
    )(first_out, own, far)


def body(queries, keys, values, rates, weights):
    own, far1, far2, far3, query_own, query_far = prepare(queries, keys, values, rates)
    own, weights = barrier((own, weights))
    got1, got2, got3 = along_x(far1, 1), along_x(far2, 2), along_x(far3, 3)
    got2, query_far, part = barrier((got2, query_far, load(weights)))
    query_far = mirror_x(query_far)
    got = [own, got1, got2, got3]
    got += [other_core(piece) for piece in got]
    parts, query_far = barrier((gradient(got, part), query_far))
    own, late_queries = reduce_rows(parts, query_own, query_far)
    pieces, first_out = gather_rows(own, queries, weights)
    matrix, shared = pack(pieces)
    shared_core = other_core(shared)
    query_own, query_core, query_far, query_far_core = late_queries
    mine, theirs = project(matrix, weights, query_own, query_far, query_core, query_far_core)
    theirs, shared_core = barrier((theirs, shared_core))
    other = other_core(theirs)
    own, far = down(mine, other, renew_third(shared, shared_core, weights))
    return finish(first_out, own, mirror_x(far))


def solution(mesh):
    in_specs = (
        P(None, ("dp", "ctx"), None),
        P(None, ("dp", "ctx"), None),
        P(None, ("dp", "ctx"), None),
        P(None, None, ("dp", "ctx")),
        P(),
    )
    out_specs = P(None, ("dp", "ctx"), None)
    return jax.shard_map(body, mesh=mesh, in_specs=in_specs, out_specs=out_specs, check_vma=False)
```

```python
import jax
import jax.numpy as jnp
from jax import lax
from jax.experimental import pallas as pl
from jax.experimental.pallas import tpu as pltpu
from jax.sharding import PartitionSpec as P

X, Z, C = 4, 8, 2
DIM, FF = 512, 1024
HALF, QUARTER = FF // 2, FF // 4
WIDE = HALF + QUARTER
ROWS = DIM // Z
BF, F32 = jnp.bfloat16, jnp.float32
upd_scale = 2.0
norm_eps = 1e-07
VMEM = pl.BlockSpec(memory_space=pltpu.VMEM)
ANY = pl.BlockSpec(memory_space=pl.ANY)
HBM = pl.BlockSpec(memory_space=pltpu.HBM)


barrier = lax.optimization_barrier


def place():
    index = lax.axis_index("ctx")
    return index // (Z * C), (index // C) % Z, index % C


def move(array, to):
    perm = []
    for x in range(X):
        for z in range(Z):
            for c in range(C):
                tx, tz, tc = to(x, z, c)
                perm.append(((x * Z + z) * C + c, (tx % X * Z + tz % Z) * C + tc % C))
    return lax.ppermute(array, "ctx", perm)


def along_x(array, distance):
    return move(array, lambda x, z, c: (x + distance, z, c))


def along_z(array, distance):
    return move(array, lambda x, z, c: (x, z + distance, c))


def opposite_z(array):
    return move(array, lambda x, z, c: (x, z + 2 - 4 * c, c))


def pair_x(array):
    return move(array, lambda x, z, c: (x ^ 1, z, c))


def mirror_x(array):
    return move(array, lambda x, z, c: (X - 1 - x, z, c))


def other_core(array):
    return move(array, lambda x, z, c: (x, z, c + 1))


def dot(left, right, dims):
    return lax.dot_general(left, right, (dims, ((), ())), preferred_element_type=F32)


def shape(*dims, dtype=BF):
    return jax.ShapeDtypeStruct(dims, dtype)


def params(mib):
    return pltpu.CompilerParams(vmem_limit_bytes=mib << 20)


def cost(flops, size):
    return pl.CostEstimate(flops=flops, bytes_accessed=size, transcendentals=0)


def at_place(start, size):
    return pl.ds(pl.multiple_of(start, size), size)


def prepare_kernel(queries, keys, values, rates, *refs):
    targets, outs, (q, k, v, r, scaled, in_sem, out_sem) = refs[:4], refs[4:6], refs[6:]
    x, _, _ = place()
    tokens = v.shape[0]
    loads = [
        pltpu.make_async_copy(source, target, in_sem.at[i])
        for i, (source, target) in enumerate(
            ((values.at[0], v), (rates, r), (keys.at[0], k), (queries.at[1], q))
        )
    ]
    for load in loads:
        load.start()
    diagonal = lax.broadcasted_iota(jnp.int32, (tokens, tokens), 0) == lax.broadcasted_iota(
        jnp.int32, (tokens, tokens), 1
    )
    heads = [lax.rem(x + distance, X) // 2 for distance in range(4)]
    copies = []

    def send(source, target):
        copy = pltpu.make_async_copy(source, target, out_sem.at[len(copies)])
        copy.start()
        copies.append(copy)

    loads[0].wait()
    loads[1].wait()
    for head in range(2):
        cols = slice(head * DIM, (head + 1) * DIM)
        row = r[0, head : head + 1, :]
        rate = jnp.sum(jnp.where(diagonal, row, 0.0), axis=1, keepdims=True)
        scaled[head] = (v[:, cols].astype(F32) * rate).astype(BF)
    for head, target in zip(heads, targets):
        send(scaled.at[head], target.at[pl.ds(tokens, tokens)])
    loads[2].wait()
    for head, target in zip(heads, targets):
        send(k.at[:, at_place(head * DIM, DIM)], target.at[pl.ds(0, tokens)])
    loads[3].wait()
    for head, target in zip((heads[0], 1 - heads[0]), outs):
        send(q.at[:, at_place(head * DIM, DIM)], target)
    for copy in copies:
        copy.wait()


def prepare(queries, keys, values, rates):
    tokens = keys.shape[1]
    pair, half = shape(2 * tokens, DIM), shape(tokens, DIM)
    wide = pltpu.VMEM((tokens, 2 * DIM), BF)
    return pl.pallas_call(
        prepare_kernel,
        out_shape=(pair, pair, pair, pair, half, half),
        in_specs=[HBM] * 4,
        out_specs=(ANY,) * 6,
        scratch_shapes=[
            wide,
            wide,
            wide,
            pltpu.VMEM(rates.shape, F32),
            pltpu.VMEM((2, tokens, DIM), BF),
            pltpu.SemaphoreType.DMA((4,)),
            pltpu.SemaphoreType.DMA((10,)),
        ],
        name="prepare",
    )(queries, keys, values, rates)


def first_kernel(queries, weights, out, q, w, sem, query_sem):
    load_query = pltpu.make_async_copy(queries.at[0], q, query_sem)
    load_query.start()
    copies = []
    for head in range(2):
        for m in range(3):
            copy = pltpu.make_async_copy(weights.at[m, head], w.at[head, m], sem.at[head, m])
            copy.start()
            copies.append(copy)
    load_query.wait()
    for head in range(2):
        cols = slice(head * DIM, (head + 1) * DIM)
        query = q[:, cols]
        copies[3 * head].wait()
        first_proj = dot(query, w[head, 0], ((1,), (0,)))
        copies[3 * head + 1].wait()
        third_proj = dot(query, w[head, 1], ((1,), (0,)))
        gated = (first_proj * jax.nn.sigmoid(first_proj) * third_proj).astype(BF)
        copies[3 * head + 2].wait()
        out[:, cols] = dot(gated, w[head, 2], ((1,), (1,))).astype(BF)


def first_block(queries, weights):
    tokens = queries.shape[1]
    return pl.pallas_call(
        first_kernel,
        out_shape=shape(tokens, 2 * DIM),
        in_specs=[HBM, HBM],
        out_specs=VMEM,
        scratch_shapes=[
            pltpu.VMEM((tokens, 2 * DIM), BF),
            pltpu.VMEM((2, 3, DIM, FF), BF),
            pltpu.SemaphoreType.DMA((2, 3)),
            pltpu.SemaphoreType.DMA,
        ],
        compiler_params=params(12),
        cost_estimate=cost(12 * tokens * DIM * FF, 7 << 20),
        name="first_block",
    )(queries, weights)


def load_kernel(weights, out, sem):
    x, _, _ = place()
    copies = []
    for m in range(3):
        copy = pltpu.make_async_copy(
            weights.at[m, x // 2, :, at_place(lax.rem(x, 2) * HALF, HALF)], out.at[m], sem.at[m]
        )
        copy.start()
        copies.append(copy)
    for copy in copies:
        copy.wait()


def load(weights):
    return pl.pallas_call(
        load_kernel,
        out_shape=shape(3, DIM, HALF),
        in_specs=[HBM],
        out_specs=VMEM,
        scratch_shapes=[pltpu.SemaphoreType.DMA((3,))],
        compiler_params=params(2),
        cost_estimate=cost(0, 3 << 20),
        name="load",
    )(weights)


def gradient_kernel(*refs):
    pieces, w = refs[:8], refs[8]
    own, up, down, keep_up, keep_down, far_up, far_down = refs[9:16]
    k, v, d, gated, total = refs[16:]
    _, z, c = place()
    tokens = pieces[0].shape[0] // 2
    for i, piece in enumerate(pieces):
        k[i * tokens : (i + 1) * tokens, :] = piece[:tokens, :]
        v[i * tokens : (i + 1) * tokens, :] = piece[tokens:, :]
    key_first = dot(k[...], w[0], ((1,), (0,)))
    key_third = dot(k[...], w[1], ((1,), (0,)))
    back_grad = -dot(v[...], w[2], ((1,), (0,)))
    sig = jax.nn.sigmoid(key_first)
    key_act = key_first * sig

    @pl.when(c == 0)
    def _():
        d[...] = (back_grad * key_third * sig * (1.0 + key_first * (1.0 - sig))).astype(BF)
        gated[...] = (key_act[:, :QUARTER] * key_third[:, :QUARTER]).astype(BF)

    @pl.when(c == 1)
    def _():
        d[...] = (back_grad * key_act).astype(BF)
        gated[...] = (key_act[:, QUARTER:] * key_third[:, QUARTER:]).astype(BF)

    total[:, :HALF] = dot(k[...], d[...], ((0,), (0,)))
    total[:, HALF:] = -dot(v[...], gated[...], ((0,), (0,)))

    def rows(distance):
        return total[at_place(lax.rem(z + distance + Z, Z) * ROWS, ROWS), :]

    own[...] = rows(0)
    up[:ROWS, :] = rows(1).astype(BF)
    up[ROWS:, :] = rows(3).astype(BF)
    down[:ROWS, :] = rows(-1).astype(BF)
    down[ROWS:, :] = rows(-3).astype(BF)
    keep_up[...] = rows(2)
    keep_down[...] = rows(-2)
    far = rows(4).astype(BF)
    far_up[...] = far[: ROWS // 2]
    far_down[...] = far[ROWS // 2 :]


def gradient(pieces, weights):
    tokens = 8 * pieces[0].shape[0] // 2
    kept, sent, half = shape(ROWS, WIDE, dtype=F32), shape(2 * ROWS, WIDE), shape(ROWS // 2, WIDE)
    return pl.pallas_call(
        gradient_kernel,
        out_shape=(kept, sent, sent, kept, kept, half, half),
        in_specs=[VMEM] * 9,
        out_specs=(VMEM,) * 7,
        scratch_shapes=[
            pltpu.VMEM((tokens, DIM), BF),
            pltpu.VMEM((tokens, DIM), BF),
            pltpu.VMEM((tokens, HALF), BF),
            pltpu.VMEM((tokens, QUARTER), BF),
            pltpu.VMEM((DIM, WIDE), F32),
        ],
        compiler_params=params(16),
        cost_estimate=cost(10 * tokens * DIM * HALF, 6 << 20),
        name="gradient",
    )(*pieces, weights)


def middle_kernel(keep_up, keep_down, got_up, got_down, far_up, far_down, up, down):
    half = ROWS // 2
    total = keep_up[...] + got_up[ROWS:, :].astype(F32)
    up[:half, :] = (total[:half] + far_up[...].astype(F32)).astype(BF)
    up[half:, :] = total[half:].astype(BF)
    total = keep_down[...] + got_down[ROWS:, :].astype(F32)
    down[:half, :] = total[:half].astype(BF)
    down[half:, :] = (total[half:] + far_down[...].astype(F32)).astype(BF)


def middle(*args):
    return pl.pallas_call(
        middle_kernel,
        out_shape=(shape(ROWS, WIDE), shape(ROWS, WIDE)),
        in_specs=[VMEM] * 6,
        out_specs=(VMEM, VMEM),
        compiler_params=params(3),
        name="middle",
    )(*args)


def total_kernel(own, a, b, c, d, out):
    total = own[...] + a[:ROWS, :].astype(F32) + b[:ROWS, :].astype(F32) + c[...].astype(F32)
    out[...] = (total + d[...].astype(F32)).astype(BF)


def add_up(*args):
    return pl.pallas_call(
        total_kernel,
        out_shape=shape(ROWS, WIDE),
        in_specs=[VMEM] * 5,
        out_specs=VMEM,
        compiler_params=params(3),
        name="add_up",
    )(*args)


def reduce_rows(parts, query_own, query_far):
    own, up, down, keep_up, keep_down, far_up, far_down = parts
    far_up, far_down = along_z(far_up, 2), along_z(far_down, -2)
    got_up, got_down = along_z(up, 1), along_z(down, -1)
    up, down = middle(keep_up, keep_down, got_up, got_down, far_up, far_down)
    up, down, query_own, query_far = barrier((up, down, query_own, query_far))
    up, down = along_z(up, 2), along_z(down, -2)
    up, down, query_core, query_far_core = barrier(
        (up, down, other_core(query_own), other_core(query_far))
    )
    return add_up(own, got_up, got_down, up, down), (query_own, query_core, query_far, query_far_core)


ORIGINS = (0, -1, 1, -2, 2, -3, 3, 4)


def gather_rows(own, queries, weights):
    own = jnp.concatenate([own, pair_x(own)], axis=1)
    own, queries = barrier((own, queries))
    up1, down1 = along_z(own, 1), along_z(own, -1)
    up2, down2 = along_z(own, 2), along_z(own, -2)
    up2, down2, first_out = barrier((up2, down2, first_block(queries, weights)))
    up3, down3 = along_z(up2, 1), along_z(down2, -1)
    _, _, c = place()
    far = opposite_z(jnp.where(c == 0, up2, down2))
    return [own, up1, down1, up2, down2, up3, down3, far], first_out


def pack_kernel(*refs):
    pieces = refs[:8]
    matrix, shared, sem = refs[8:]
    x, z, _ = place()
    copies = []
    for i, piece in enumerate(pieces):
        rows = at_place(lax.rem(z + ORIGINS[i] + Z, Z) * ROWS, ROWS)
        for j in range(4):
            side = lax.rem(x + j // 2, 2)
            target, size, offset = ((matrix, HALF, 0), (shared, QUARTER, HALF))[j % 2]
            copy = pltpu.make_async_copy(
                piece.at[:, pl.ds(j // 2 * WIDE + offset, size)],
                target.at[rows, at_place(side * size, size)],
                sem.at[i, j],
            )
            copy.start()
            copies.append(copy)
    for copy in copies:
        copy.wait()


def pack(pieces):
    return pl.pallas_call(
        pack_kernel,
        out_shape=(shape(DIM, FF), shape(DIM, HALF)),
        in_specs=[ANY] * 8,
        out_specs=(VMEM, VMEM),
        scratch_shapes=[pltpu.SemaphoreType.DMA((8, 4))],
        compiler_params=params(4),
        cost_estimate=cost(0, 3 << 20),
        name="pack",
    )(*pieces)


def diagonal(value):
    return jnp.where(
        lax.broadcasted_iota(jnp.int32, (DIM, DIM), 0)
        == lax.broadcasted_iota(jnp.int32, (DIM, DIM), 1),
        value,
        0.0,
    )


def gram_of(*parts):
    gram = dot(parts[0], parts[0], ((1,), (1,)))
    for part in parts[1:]:
        gram += dot(part, part, ((1,), (1,)))
    gram = gram.astype(BF)
    gram_float = gram.astype(F32)
    level = jnp.sqrt(jnp.sum(gram_float * gram_float, keepdims=True)) + norm_eps
    half = 0.5 / level
    first_poly = (diagonal(1.5) - gram_float * half).astype(BF)
    return gram, first_poly, half, upd_scale / jnp.sqrt(level)


def combine(gram, first_poly, half):
    squared = dot(first_poly, first_poly, ((1,), (0,))).astype(BF)
    moved = dot(squared, gram, ((1,), (0,)))
    second_poly = (diagonal(1.5) - moved * half).astype(BF)
    return dot(second_poly, first_poly, ((1,), (0,))).astype(BF)


def project_kernel(scaled, weights, query_own, query_far, query_core, query_far_core, *refs):
    mine, theirs, w, q, sem = refs
    x, _, c = place()
    load = pltpu.make_async_copy(weights.at[c, x // 2], w, sem)
    load.start()
    tokens = query_own.shape[0]
    for i, query in enumerate((query_own, query_far, query_core, query_far_core)):
        q[i * tokens : (i + 1) * tokens, :] = query[...]
    gram, first_poly, half, factor = gram_of(scaled[...])
    combined = combine(gram, first_poly, half)
    update = dot(combined, scaled[...], ((1,), (0,))) * factor
    load.wait()
    renewed = (w[...].astype(F32) - update).astype(BF)
    projected = dot(q[...], renewed, ((1,), (0,)))
    mine[...] = projected[: 2 * tokens]
    theirs[...] = projected[2 * tokens :]


def project(scaled, weights, *queries):
    tokens = queries[0].shape[0]
    half = shape(2 * tokens, FF, dtype=F32)
    return pl.pallas_call(
        project_kernel,
        out_shape=(half, half),
        in_specs=[VMEM, HBM] + [VMEM] * 4,
        out_specs=(VMEM, VMEM),
        scratch_shapes=[
            pltpu.VMEM((DIM, FF), BF),
            pltpu.VMEM((4 * tokens, DIM), BF),
            pltpu.SemaphoreType.DMA,
        ],
        compiler_params=params(16),
        cost_estimate=cost(22 * 10**8, 5 << 20),
        name="project",
    )(scaled, weights, *queries)


def third_kernel(mine, other, weights, out, w, sem):
    x, _, c = place()
    load = pltpu.make_async_copy(weights.at[2, x // 2], w, sem)
    load.start()
    gram, first_poly, half, factor = gram_of(mine[...], other[...])
    combined = combine(gram, first_poly, half)
    load.wait()
    for core, part in ((c, mine), (1 - c, other)):
        update = dot(combined, part[...], ((1,), (0,))) * factor
        for side in range(2):
            cols = at_place(side * HALF + core * QUARTER, QUARTER)
            change = update[:, side * QUARTER : (side + 1) * QUARTER]
            out[:, cols] = (w[:, cols].astype(F32) - change).astype(BF)


def renew_third(mine, other, weights):
    return pl.pallas_call(
        third_kernel,
        out_shape=shape(DIM, FF),
        in_specs=[VMEM, VMEM, HBM],
        out_specs=VMEM,
        scratch_shapes=[
            pltpu.VMEM((DIM, FF), BF),
            pltpu.SemaphoreType.DMA,
        ],
        compiler_params=params(16),
        cost_estimate=cost(19 * 10**8, 4 << 20),
        name="renew_third",
    )(mine, other, weights)


def down_kernel(mine, other, weights, own, far, gated):
    _, _, c = place()

    @pl.when(c == 0)
    def _():
        first_proj = mine[...]
        gated[...] = (first_proj * jax.nn.sigmoid(first_proj) * other[...]).astype(BF)

    @pl.when(c == 1)
    def _():
        first_proj = other[...]
        gated[...] = (first_proj * jax.nn.sigmoid(first_proj) * mine[...]).astype(BF)

    result = dot(gated[...], weights[...], ((1,), (1,))).astype(BF)
    tokens = own.shape[0]
    own[...] = result[:tokens]
    far[...] = result[tokens:]


def down(mine, other, weights):
    tokens = mine.shape[0] // 2
    part = shape(tokens, DIM)
    return pl.pallas_call(
        down_kernel,
        out_shape=(part, part),
        in_specs=[VMEM] * 3,
        out_specs=(VMEM, VMEM),
        scratch_shapes=[pltpu.VMEM((2 * tokens, FF), BF)],
        compiler_params=params(8),
        cost_estimate=cost(3 * 10**8, 3 << 20),
        name="down",
    )(mine, other, weights)


def finish_kernel(first_out, own, far, out):
    x, _, _ = place()
    out[0] = first_out[...]
    out[1, :, at_place(x // 2 * DIM, DIM)] = own[...]
    out[1, :, at_place((1 - x // 2) * DIM, DIM)] = far[...]


def finish(first_out, own, far):
    return pl.pallas_call(
        finish_kernel,
        out_shape=shape(2, *first_out.shape),
        in_specs=[VMEM] * 3,
        out_specs=VMEM,
        compiler_params=params(2),
        name="finish",
    )(first_out, own, far)


def body(queries, keys, values, rates, weights):
    own, far1, far2, far3, query_own, query_far = prepare(queries, keys, values, rates)
    own, weights = barrier((own, weights))
    got1, got2, got3 = along_x(far1, 1), along_x(far2, 2), along_x(far3, 3)
    got2, query_far, part = barrier((got2, query_far, load(weights)))
    query_far = mirror_x(query_far)
    got = [own, got1, got2, got3]
    got += [other_core(piece) for piece in got]
    parts, query_far = barrier((gradient(got, part), query_far))
    own, late_queries = reduce_rows(parts, query_own, query_far)
    pieces, first_out = gather_rows(own, queries, weights)
    matrix, shared = pack(pieces)
    shared_core = other_core(shared)
    query_own, query_core, query_far, query_far_core = late_queries
    mine, theirs = project(matrix, weights, query_own, query_far, query_core, query_far_core)
    theirs, shared_core = barrier((theirs, shared_core))
    other = other_core(theirs)
    own, far = down(mine, other, renew_third(shared, shared_core, weights))
    return finish(first_out, own, mirror_x(far))


def solution(mesh):
    in_specs = (
        P(None, ("dp", "ctx"), None),
        P(None, ("dp", "ctx"), None),
        P(None, ("dp", "ctx"), None),
        P(None, None, ("dp", "ctx")),
        P(),
    )
    out_specs = P(None, ("dp", "ctx"), None)
    return jax.shard_map(body, mesh=mesh, in_specs=in_specs, out_specs=out_specs, check_vma=False)
```

```python
import jax
import jax.numpy as jnp
from jax import lax
from jax.experimental import pallas as pl
from jax.experimental.pallas import tpu as pltpu
from jax.sharding import PartitionSpec as P

X, Z, C = 4, 8, 2
DIM, FF = 512, 1024
HALF, QUARTER = FF // 2, FF // 4
WIDE = HALF + QUARTER
ROWS = DIM // Z
BF, F32 = jnp.bfloat16, jnp.float32
upd_scale = 2.0
norm_eps = 1e-07
VMEM = pl.BlockSpec(memory_space=pltpu.VMEM)
ANY = pl.BlockSpec(memory_space=pl.ANY)
HBM = pl.BlockSpec(memory_space=pltpu.HBM)


barrier = lax.optimization_barrier


def place():
    index = lax.axis_index("ctx")
    return index // (Z * C), (index // C) % Z, index % C


def move(array, to):
    perm = []
    for x in range(X):
        for z in range(Z):
            for c in range(C):
                tx, tz, tc = to(x, z, c)
                perm.append(((x * Z + z) * C + c, (tx % X * Z + tz % Z) * C + tc % C))
    return lax.ppermute(array, "ctx", perm)


def along_x(array, distance):
    return move(array, lambda x, z, c: (x + distance, z, c))


def along_z(array, distance):
    return move(array, lambda x, z, c: (x, z + distance, c))


def opposite_z(array):
    return move(array, lambda x, z, c: (x, z + 2 - 4 * c, c))


def pair_x(array):
    return move(array, lambda x, z, c: (x ^ 1, z, c))


def mirror_x(array):
    return move(array, lambda x, z, c: (X - 1 - x, z, c))


def other_core(array):
    return move(array, lambda x, z, c: (x, z, c + 1))


def dot(left, right, dims):
    return lax.dot_general(left, right, (dims, ((), ())), preferred_element_type=F32)


def shape(*dims, dtype=BF):
    return jax.ShapeDtypeStruct(dims, dtype)


def params(mib):
    return pltpu.CompilerParams(vmem_limit_bytes=mib << 20)


def cost(flops, size):
    return pl.CostEstimate(flops=flops, bytes_accessed=size, transcendentals=0)


def at_place(start, size):
    return pl.ds(pl.multiple_of(start, size), size)


def prepare_kernel(queries, keys, values, rates, *refs):
    targets, outs, (q, k, v, r, scaled, in_sem, out_sem) = refs[:4], refs[4:6], refs[6:]
    x, _, _ = place()
    tokens = v.shape[0]
    loads = [
        pltpu.make_async_copy(source, target, in_sem.at[i])
        for i, (source, target) in enumerate(
            ((values.at[0], v), (rates, r), (keys.at[0], k), (queries.at[1], q))
        )
    ]
    for load in loads:
        load.start()
    diagonal = lax.broadcasted_iota(jnp.int32, (tokens, tokens), 0) == lax.broadcasted_iota(
        jnp.int32, (tokens, tokens), 1
    )
    heads = [lax.rem(x + distance, X) // 2 for distance in range(4)]
    copies = []

    def send(source, target):
        copy = pltpu.make_async_copy(source, target, out_sem.at[len(copies)])
        copy.start()
        copies.append(copy)

    loads[0].wait()
    loads[1].wait()
    for head in range(2):
        cols = slice(head * DIM, (head + 1) * DIM)
        row = r[0, head : head + 1, :]
        rate = jnp.sum(jnp.where(diagonal, row, 0.0), axis=1, keepdims=True)
        scaled[head] = (v[:, cols].astype(F32) * rate).astype(BF)
    for head, target in zip(heads, targets):
        send(scaled.at[head], target.at[pl.ds(tokens, tokens)])
    loads[2].wait()
    for head, target in zip(heads, targets):
        send(k.at[:, at_place(head * DIM, DIM)], target.at[pl.ds(0, tokens)])
    loads[3].wait()
    for head, target in zip((heads[0], 1 - heads[0]), outs):
        send(q.at[:, at_place(head * DIM, DIM)], target)
    for copy in copies:
        copy.wait()


def prepare(queries, keys, values, rates):
    tokens = keys.shape[1]
    pair, half = shape(2 * tokens, DIM), shape(tokens, DIM)
    wide = pltpu.VMEM((tokens, 2 * DIM), BF)
    return pl.pallas_call(
        prepare_kernel,
        out_shape=(pair, pair, pair, pair, half, half),
        in_specs=[HBM] * 4,
        out_specs=(ANY,) * 6,
        scratch_shapes=[
            wide,
            wide,
            wide,
            pltpu.VMEM(rates.shape, F32),
            pltpu.VMEM((2, tokens, DIM), BF),
            pltpu.SemaphoreType.DMA((4,)),
            pltpu.SemaphoreType.DMA((10,)),
        ],
        name="prepare",
    )(queries, keys, values, rates)


def first_kernel(queries, weights, out, q, w, sem, query_sem):
    load_query = pltpu.make_async_copy(queries.at[0], q, query_sem)
    load_query.start()
    copies = []
    for head in range(2):
        for m in range(3):
            copy = pltpu.make_async_copy(weights.at[m, head], w.at[head, m], sem.at[head, m])
            copy.start()
            copies.append(copy)
    load_query.wait()
    for head in range(2):
        cols = slice(head * DIM, (head + 1) * DIM)
        query = q[:, cols]
        copies[3 * head].wait()
        first_proj = dot(query, w[head, 0], ((1,), (0,)))
        copies[3 * head + 1].wait()
        third_proj = dot(query, w[head, 1], ((1,), (0,)))
        gated = (first_proj * jax.nn.sigmoid(first_proj) * third_proj).astype(BF)
        copies[3 * head + 2].wait()
        out[:, cols] = dot(gated, w[head, 2], ((1,), (1,))).astype(BF)


def first_block(queries, weights):
    tokens = queries.shape[1]
    return pl.pallas_call(
        first_kernel,
        out_shape=shape(tokens, 2 * DIM),
        in_specs=[HBM, HBM],
        out_specs=VMEM,
        scratch_shapes=[
            pltpu.VMEM((tokens, 2 * DIM), BF),
            pltpu.VMEM((2, 3, DIM, FF), BF),
            pltpu.SemaphoreType.DMA((2, 3)),
            pltpu.SemaphoreType.DMA,
        ],
        compiler_params=params(48),
        cost_estimate=cost(12 * tokens * DIM * FF, 7 << 20),
        name="first_block",
    )(queries, weights)


def load_kernel(weights, out, sem):
    x, _, _ = place()
    copies = []
    for m in range(3):
        copy = pltpu.make_async_copy(
            weights.at[m, x // 2, :, at_place(lax.rem(x, 2) * HALF, HALF)], out.at[m], sem.at[m]
        )
        copy.start()
        copies.append(copy)
    for copy in copies:
        copy.wait()


def load(weights):
    return pl.pallas_call(
        load_kernel,
        out_shape=shape(3, DIM, HALF),
        in_specs=[HBM],
        out_specs=VMEM,
        scratch_shapes=[pltpu.SemaphoreType.DMA((3,))],
        compiler_params=params(2),
        cost_estimate=cost(0, 3 << 20),
        name="load",
    )(weights)


def gradient_kernel(*refs):
    pieces, w = refs[:8], refs[8]
    own, up, down, keep_up, keep_down, far_up, far_down = refs[9:16]
    k, v, d, gated, total = refs[16:]
    _, z, c = place()
    tokens = pieces[0].shape[0] // 2
    for i, piece in enumerate(pieces):
        k[i * tokens : (i + 1) * tokens, :] = piece[:tokens, :]
        v[i * tokens : (i + 1) * tokens, :] = piece[tokens:, :]
    key_first = dot(k[...], w[0], ((1,), (0,)))
    key_third = dot(k[...], w[1], ((1,), (0,)))
    back_grad = -dot(v[...], w[2], ((1,), (0,)))
    sig = jax.nn.sigmoid(key_first)
    key_act = key_first * sig

    @pl.when(c == 0)
    def _():
        d[...] = (back_grad * key_third * sig * (1.0 + key_first * (1.0 - sig))).astype(BF)
        gated[...] = (key_act[:, :QUARTER] * key_third[:, :QUARTER]).astype(BF)

    @pl.when(c == 1)
    def _():
        d[...] = (back_grad * key_act).astype(BF)
        gated[...] = (key_act[:, QUARTER:] * key_third[:, QUARTER:]).astype(BF)

    total[:, :HALF] = dot(k[...], d[...], ((0,), (0,)))
    total[:, HALF:] = -dot(v[...], gated[...], ((0,), (0,)))

    def rows(distance):
        return total[at_place(lax.rem(z + distance + Z, Z) * ROWS, ROWS), :]

    own[...] = rows(0)
    up[:ROWS, :] = rows(1).astype(BF)
    up[ROWS:, :] = rows(3).astype(BF)
    down[:ROWS, :] = rows(-1).astype(BF)
    down[ROWS:, :] = rows(-3).astype(BF)
    keep_up[...] = rows(2)
    keep_down[...] = rows(-2)
    far = rows(4).astype(BF)
    far_up[...] = far[: ROWS // 2]
    far_down[...] = far[ROWS // 2 :]


def gradient(pieces, weights):
    tokens = 8 * pieces[0].shape[0] // 2
    kept, sent, half = shape(ROWS, WIDE, dtype=F32), shape(2 * ROWS, WIDE), shape(ROWS // 2, WIDE)
    return pl.pallas_call(
        gradient_kernel,
        out_shape=(kept, sent, sent, kept, kept, half, half),
        in_specs=[VMEM] * 9,
        out_specs=(VMEM,) * 7,
        scratch_shapes=[
            pltpu.VMEM((tokens, DIM), BF),
            pltpu.VMEM((tokens, DIM), BF),
            pltpu.VMEM((tokens, HALF), BF),
            pltpu.VMEM((tokens, QUARTER), BF),
            pltpu.VMEM((DIM, WIDE), F32),
        ],
        compiler_params=params(16),
        cost_estimate=cost(10 * tokens * DIM * HALF, 6 << 20),
        name="gradient",
    )(*pieces, weights)


def middle_kernel(keep_up, keep_down, got_up, got_down, far_up, far_down, up, down):
    half = ROWS // 2
    total = keep_up[...] + got_up[ROWS:, :].astype(F32)
    up[:half, :] = (total[:half] + far_up[...].astype(F32)).astype(BF)
    up[half:, :] = total[half:].astype(BF)
    total = keep_down[...] + got_down[ROWS:, :].astype(F32)
    down[:half, :] = total[:half].astype(BF)
    down[half:, :] = (total[half:] + far_down[...].astype(F32)).astype(BF)


def middle(*args):
    return pl.pallas_call(
        middle_kernel,
        out_shape=(shape(ROWS, WIDE), shape(ROWS, WIDE)),
        in_specs=[VMEM] * 6,
        out_specs=(VMEM, VMEM),
        compiler_params=params(3),
        name="middle",
    )(*args)


def total_kernel(own, a, b, c, d, out):
    total = own[...] + a[:ROWS, :].astype(F32) + b[:ROWS, :].astype(F32) + c[...].astype(F32)
    out[...] = (total + d[...].astype(F32)).astype(BF)


def add_up(*args):
    return pl.pallas_call(
        total_kernel,
        out_shape=shape(ROWS, WIDE),
        in_specs=[VMEM] * 5,
        out_specs=VMEM,
        compiler_params=params(3),
        name="add_up",
    )(*args)


def reduce_rows(parts, query_own, query_far):
    own, up, down, keep_up, keep_down, far_up, far_down = parts
    far_up, far_down = along_z(far_up, 2), along_z(far_down, -2)
    got_up, got_down = along_z(up, 1), along_z(down, -1)
    up, down = middle(keep_up, keep_down, got_up, got_down, far_up, far_down)
    up, down, query_own, query_far = barrier((up, down, query_own, query_far))
    up, down = along_z(up, 2), along_z(down, -2)
    up, down, query_core, query_far_core = barrier(
        (up, down, other_core(query_own), other_core(query_far))
    )
    return add_up(own, got_up, got_down, up, down), (query_own, query_core, query_far, query_far_core)


ORIGINS = (0, -1, 1, -2, 2, -3, 3, 4)


def gather_rows(own, queries, weights):
    own = jnp.concatenate([own, pair_x(own)], axis=1)
    own, queries = barrier((own, queries))
    up1, down1 = along_z(own, 1), along_z(own, -1)
    up2, down2 = along_z(own, 2), along_z(own, -2)
    up2, down2, first_out = barrier((up2, down2, first_block(queries, weights)))
    up3, down3 = along_z(up2, 1), along_z(down2, -1)
    _, _, c = place()
    far = opposite_z(jnp.where(c == 0, up2, down2))
    return [own, up1, down1, up2, down2, up3, down3, far], first_out


def pack_kernel(*refs):
    pieces = refs[:8]
    matrix, shared, sem = refs[8:]
    x, z, _ = place()
    copies = []
    for i, piece in enumerate(pieces):
        rows = at_place(lax.rem(z + ORIGINS[i] + Z, Z) * ROWS, ROWS)
        for j in range(4):
            side = lax.rem(x + j // 2, 2)
            target, size, offset = ((matrix, HALF, 0), (shared, QUARTER, HALF))[j % 2]
            copy = pltpu.make_async_copy(
                piece.at[:, pl.ds(j // 2 * WIDE + offset, size)],
                target.at[rows, at_place(side * size, size)],
                sem.at[i, j],
            )
            copy.start()
            copies.append(copy)
    for copy in copies:
        copy.wait()


def pack(pieces):
    return pl.pallas_call(
        pack_kernel,
        out_shape=(shape(DIM, FF), shape(DIM, HALF)),
        in_specs=[ANY] * 8,
        out_specs=(VMEM, VMEM),
        scratch_shapes=[pltpu.SemaphoreType.DMA((8, 4))],
        compiler_params=params(4),
        cost_estimate=cost(0, 3 << 20),
        name="pack",
    )(*pieces)


def diagonal(value):
    return jnp.where(
        lax.broadcasted_iota(jnp.int32, (DIM, DIM), 0)
        == lax.broadcasted_iota(jnp.int32, (DIM, DIM), 1),
        value,
        0.0,
    )


def gram_of(*parts):
    gram = dot(parts[0], parts[0], ((1,), (1,)))
    for part in parts[1:]:
        gram += dot(part, part, ((1,), (1,)))
    gram = gram.astype(BF)
    gram_float = gram.astype(F32)
    level = jnp.sqrt(jnp.sum(gram_float * gram_float, keepdims=True)) + norm_eps
    half = 0.5 / level
    first_poly = (diagonal(1.5) - gram_float * half).astype(BF)
    return gram, first_poly, half, upd_scale / jnp.sqrt(level)


def combine(gram, first_poly, half):
    squared = dot(first_poly, first_poly, ((1,), (0,))).astype(BF)
    moved = dot(squared, gram, ((1,), (0,)))
    second_poly = (diagonal(1.5) - moved * half).astype(BF)
    return dot(second_poly, first_poly, ((1,), (0,))).astype(BF)


def project_kernel(scaled, weights, query_own, query_far, query_core, query_far_core, *refs):
    mine, theirs, w, q, sem = refs
    x, _, c = place()
    load = pltpu.make_async_copy(weights.at[c, x // 2], w, sem)
    load.start()
    tokens = query_own.shape[0]
    for i, query in enumerate((query_own, query_far, query_core, query_far_core)):
        q[i * tokens : (i + 1) * tokens, :] = query[...]
    gram, first_poly, half, factor = gram_of(scaled[...])
    combined = combine(gram, first_poly, half)
    update = dot(combined, scaled[...], ((1,), (0,))) * factor
    load.wait()
    renewed = (w[...].astype(F32) - update).astype(BF)
    projected = dot(q[...], renewed, ((1,), (0,)))
    mine[...] = projected[: 2 * tokens]
    theirs[...] = projected[2 * tokens :]


def project(scaled, weights, *queries):
    tokens = queries[0].shape[0]
    half = shape(2 * tokens, FF, dtype=F32)
    return pl.pallas_call(
        project_kernel,
        out_shape=(half, half),
        in_specs=[VMEM, HBM] + [VMEM] * 4,
        out_specs=(VMEM, VMEM),
        scratch_shapes=[
            pltpu.VMEM((DIM, FF), BF),
            pltpu.VMEM((4 * tokens, DIM), BF),
            pltpu.SemaphoreType.DMA,
        ],
        compiler_params=params(16),
        cost_estimate=cost(22 * 10**8, 5 << 20),
        name="project",
    )(scaled, weights, *queries)


def third_kernel(mine, other, weights, out, w, sem):
    x, _, c = place()
    load = pltpu.make_async_copy(weights.at[2, x // 2], w, sem)
    load.start()
    gram, first_poly, half, factor = gram_of(mine[...], other[...])
    combined = combine(gram, first_poly, half)
    load.wait()
    for core, part in ((c, mine), (1 - c, other)):
        update = dot(combined, part[...], ((1,), (0,))) * factor
        for side in range(2):
            cols = at_place(side * HALF + core * QUARTER, QUARTER)
            change = update[:, side * QUARTER : (side + 1) * QUARTER]
            out[:, cols] = (w[:, cols].astype(F32) - change).astype(BF)


def renew_third(mine, other, weights):
    return pl.pallas_call(
        third_kernel,
        out_shape=shape(DIM, FF),
        in_specs=[VMEM, VMEM, HBM],
        out_specs=VMEM,
        scratch_shapes=[
            pltpu.VMEM((DIM, FF), BF),
            pltpu.SemaphoreType.DMA,
        ],
        compiler_params=params(16),
        cost_estimate=cost(19 * 10**8, 4 << 20),
        name="renew_third",
    )(mine, other, weights)


def down_kernel(mine, other, weights, own, far, gated):
    _, _, c = place()

    @pl.when(c == 0)
    def _():
        first_proj = mine[...]
        gated[...] = (first_proj * jax.nn.sigmoid(first_proj) * other[...]).astype(BF)

    @pl.when(c == 1)
    def _():
        first_proj = other[...]
        gated[...] = (first_proj * jax.nn.sigmoid(first_proj) * mine[...]).astype(BF)

    result = dot(gated[...], weights[...], ((1,), (1,))).astype(BF)
    tokens = own.shape[0]
    own[...] = result[:tokens]
    far[...] = result[tokens:]


def down(mine, other, weights):
    tokens = mine.shape[0] // 2
    part = shape(tokens, DIM)
    return pl.pallas_call(
        down_kernel,
        out_shape=(part, part),
        in_specs=[VMEM] * 3,
        out_specs=(VMEM, VMEM),
        scratch_shapes=[pltpu.VMEM((2 * tokens, FF), BF)],
        compiler_params=params(8),
        cost_estimate=cost(3 * 10**8, 3 << 20),
        name="down",
    )(mine, other, weights)


def finish_kernel(first_out, own, far, out):
    x, _, _ = place()
    out[0] = first_out[...]
    out[1, :, at_place(x // 2 * DIM, DIM)] = own[...]
    out[1, :, at_place((1 - x // 2) * DIM, DIM)] = far[...]


def finish(first_out, own, far):
    return pl.pallas_call(
        finish_kernel,
        out_shape=shape(2, *first_out.shape),
        in_specs=[VMEM] * 3,
        out_specs=VMEM,
        compiler_params=params(2),
        name="finish",
    )(first_out, own, far)


def body(queries, keys, values, rates, weights):
    own, far1, far2, far3, query_own, query_far = prepare(queries, keys, values, rates)
    own, weights = barrier((own, weights))
    got1, got2, got3 = along_x(far1, 1), along_x(far2, 2), along_x(far3, 3)
    got2, query_far, part = barrier((got2, query_far, load(weights)))
    query_far = mirror_x(query_far)
    got = [own, got1, got2, got3]
    got += [other_core(piece) for piece in got]
    parts, query_far = barrier((gradient(got, part), query_far))
    own, late_queries = reduce_rows(parts, query_own, query_far)
    pieces, first_out = gather_rows(own, queries, weights)
    matrix, shared = pack(pieces)
    shared_core = other_core(shared)
    query_own, query_core, query_far, query_far_core = late_queries
    mine, theirs = project(matrix, weights, query_own, query_far, query_core, query_far_core)
    theirs, shared_core = barrier((theirs, shared_core))
    other = other_core(theirs)
    own, far = down(mine, other, renew_third(shared, shared_core, weights))
    return finish(first_out, own, mirror_x(far))


def solution(mesh):
    in_specs = (
        P(None, ("dp", "ctx"), None),
        P(None, ("dp", "ctx"), None),
        P(None, ("dp", "ctx"), None),
        P(None, None, ("dp", "ctx")),
        P(),
    )
    out_specs = P(None, ("dp", "ctx"), None)
    return jax.shard_map(body, mesh=mesh, in_specs=in_specs, out_specs=out_specs, check_vma=False)
```
